32 devices in a mesh: rep: 2 (over y), exp: 16 (over z, x, core).
Axes of the slice: x: 2, y: 2, z: 4, core: 2. Of those that a mesh axis runs over, the one named last changes fastest.
Arguments:
- cache_keys: bfloat16 [32, 2048, 512], P(('rep', 'exp')), may hold values from -6.5 to 6.5
- cache_values: bfloat16 [32, 2048, 512], P(('rep', 'exp')), may hold values from -6 to 6
- lengths: int32 [32], P(('rep', 'exp')), may hold values from 512 to 2048, as said below
- drift_rows: int32 [2, 32, 8], P(None, ('rep', 'exp')), may hold values from 0 to 2047, as said below
- block_in: bfloat16 [32, 8, 4096], P(('rep', 'exp')), may hold values from -6 to 6
- drift_in: bfloat16 [2, 32, 8, 4096], P(None, ('rep', 'exp')), may hold values from -6 to 6
- queries: bfloat16 [2, 32, 16, 4096], P(None, ('rep', 'exp')), may hold values from -150 to 150
- new_keys: bfloat16 [2, 32, 16, 512], P(None, ('rep', 'exp')), may hold values from -6 to 6
- new_values: bfloat16 [2, 32, 16, 512], P(None, ('rep', 'exp')), may hold values from -6 to 6
- norm_gain: float32 [4096], replicated, may hold values from 0.25 to 1.75
- expert_ids: int32 [2, 32, 16, 8], P(None, ('rep', 'exp')), may hold values from 0 to 15, all different within a row; in each aligned block of 16 rows (0 to 15, 16 to 31, ..., all dimensions but the last counted through in order) at most 12 rows name the same one
- gate_weights: bfloat16 [2, 32, 16, 8], P(None, ('rep', 'exp')), may hold values from 0.049804688 to 0.3984375
- w_gate: bfloat16 [16, 4096, 1024], P('exp', None, 'rep'), may hold values from -0.09375 to 0.09375
- w_up: bfloat16 [16, 4096, 1024], P('exp', None, 'rep'), may hold values from -0.09375 to 0.09375
- w_down: bfloat16 [16, 1024, 4096], P('exp', 'rep'), may hold values from -0.1875 to 0.1875
Outputs:
- out: bfloat16 [2, 32, 16, 4096], P(None, ('rep', 'exp'))
The draws below stay inside these ranges and needn't reach their ends.
Inputs may be any that keep to these rules, and one draw needn't show every extreme that they name: `lengths`: one request has exactly 2048. `drift_rows`: for each step and request, 8 different positions in increasing order, all below that request's length. `expert_ids`: each row names 8 different experts; within one step the rows of one request name any expert at most 12 times, a bound that some block reaches.
All inputs are finite; a program needn't handle non-finite values.
Results may differ from the reference program's by a relative error of at most 0.012.
Values may be sent and summed in bfloat16 or wider, within the bound.
A program may use at most 128 MiB of HBM per device.

```python
import math
import jax
import jax.numpy as jnp
import numpy as np
from jax import lax

D = 4096
H = 32
KVH = 4
HD = 128
FFE = 1024
TOP = 8
BLOCK = 8
DRIFT = 8
CACHE = 2048
ROWS = 16
REQUESTS = 32
EXPERTS = 16
CAP = 12
N_REP = 2


def length_table(key):
    lengths_drawn = jax.random.randint(jax.random.fold_in(key, 11), (REQUESTS,), CACHE // 4, CACHE + 1)
    longest = jax.random.randint(jax.random.fold_in(key, 12), (), 0, REQUESTS)
    return jnp.where(jnp.arange(REQUESTS) == longest, CACHE, lengths_drawn).astype(jnp.int32)


def draw_lengths(key, part):
    return length_table(key)


def draw_drift_rows(key, part):
    length_all = length_table(key)
    offsets = jax.random.randint(jax.random.fold_in(key, 13), (2, REQUESTS, DRIFT), 0, 1048576)
    stratum = jnp.arange(DRIFT)[None, None, :]
    stratum_low = length_all[None, :, None] * stratum // DRIFT
    stratum_high = length_all[None, :, None] * (stratum + 1) // DRIFT
    return (stratum_low + offsets % (stratum_high - stratum_low)).astype(jnp.int32)


def key_table(key):
    normal_draw = jax.random.normal(jax.random.fold_in(key, 21), (REQUESTS, CACHE, KVH * HD), jnp.float32)
    normal_draw = jnp.clip(normal_draw, -6.0, 6.0)
    return normal_draw


def draw_cache_keys(key, part):
    return key_table(key).astype(jnp.bfloat16)


def draw_queries(key, part):
    normal_draw = jax.random.normal(jax.random.fold_in(key, 31), (2, REQUESTS, ROWS, H * HD), jnp.float32)
    normal_draw = jnp.clip(normal_draw, -6.0, 6.0)
    return normal_draw.astype(jnp.bfloat16)


def level_of(rng, extent, split, least, high):
    level = 1.0
    for dim, shards_of in split:
        heights = jax.random.uniform(jax.random.fold_in(jax.random.fold_in(rng, 6), dim), (shards_of,), jnp.float32, least / len(split), high / len(split))
        level = level * jnp.repeat(jnp.exp(heights), extent[dim] // shards_of).reshape((-1,) + (1,) * (len(extent) - 1 - dim))
    return level


def assign_block(rng, own, number, rows, count, top, limit, skew):
    sequence = jax.random.permutation(rng, count)
    heavy_load, usual = portions_of(count, rows * top, limit, skew, True), portions_of(count, rows * top, limit, skew, False)
    places = jnp.arange(count)

    def named(sizes, rotation):
        used = int((sizes > 0).sum())
        fixed = max(1, used // 4)
        moved = fixed + (places - fixed + rotation * (used - fixed)) % max(1, count - fixed)
        return jnp.zeros((count,), jnp.int32).at[sequence[jnp.where(places < fixed, places, moved)]].set(jnp.asarray(sizes, jnp.int32))

    sizes = jnp.where(number % 4 == 0, named(heavy_load, number // 4), named(usual, number - number // 4 - 1))
    mixed = jax.random.permutation(jax.random.fold_in(own, 3), count)
    source_of, taker = mixed[0:count // 2 * 2:2], mixed[1:count // 2 * 2:2]
    margin = jnp.minimum(sizes[source_of] - 1, limit - sizes[taker]) // 2
    margin = jnp.where((source_of == sequence[0]) | (taker == sequence[0]) | (sizes[taker] == 0), 0, jnp.maximum(margin, 0))
    moved = jax.random.randint(jax.random.fold_in(own, 4), (count // 2,), 0, 1 << 20) % (margin + 1)
    sizes = sizes.at[source_of].add(-moved).at[taker].add(moved)
    labels = jnp.searchsorted(jnp.cumsum(sizes), jnp.arange(rows * top), side="right").astype(jnp.int32)
    grid = labels.reshape(top, rows).T
    grid = grid[jax.random.permutation(jax.random.fold_in(own, 1), rows)]
    rotation = jax.random.randint(jax.random.fold_in(own, 2), (rows, 1), 0, top)
    return jnp.take_along_axis(grid, (jnp.arange(top)[None, :] + rotation) % top, axis=1)


def portions_of(count, total, bound, skew, full):
    weights = [(1 << 20) // math.isqrt(standing ** skew) + 1 for standing in range(1, count + 1)]
    largest = bound if full else min(bound, max(-(-total // count), total * weights[0] // sum(weights)))
    least = 1 if total - largest >= count - 1 else 0
    given, surplus = [largest] + [least] * (count - 1), total - largest - least * (count - 1)
    while surplus > 0:
        free = [i for i in range(1, count) if given[i] < largest] or [i for i in range(1, count) if given[i] < bound]
        mass, budget = sum([weights[i] for i in free]), surplus
        for i in free:
            more = min(bound - given[i], max(1, budget * weights[i] // mass), surplus)
            given[i] = given[i] + more
            surplus = surplus - more
    return np.array(given)


def bell_draw(rng, shape, scale, reach, shards=(), dtype=jnp.bfloat16):
    values = jax.random.normal(rng, shape, jnp.float32) * scale
    if len(shards) > 0:
        values = level_of(rng, shape, shards, -0.22, 0.18) * values
    return jnp.clip(values, min=-reach, max=reach).astype(dtype)


def setup_inputs(seed: int = 0) -> dict:
    arg_keys = jax.random.split(jax.random.key(seed), 16)
    cache_keys = draw_cache_keys(jax.random.fold_in(arg_keys[15], 71), 0)
    cache_values = bell_draw(arg_keys[1], (REQUESTS, CACHE, KVH * HD), 1.0, 6.0, ((0, 32),))
    lengths = draw_lengths(jax.random.fold_in(arg_keys[15], 71), 0)
    drift_rows = draw_drift_rows(jax.random.fold_in(arg_keys[15], 71), 0)
    block_in = bell_draw(arg_keys[4], (REQUESTS, BLOCK, D), 1.0, 6.0, ((0, 32),))
    drift_in = bell_draw(arg_keys[5], (2, REQUESTS, DRIFT, D), 1.0, 6.0, ((1, 32),))
    queries = draw_queries(jax.random.fold_in(arg_keys[15], 71), 0)
    new_keys = bell_draw(arg_keys[7], (2, REQUESTS, ROWS, KVH * HD), 1.0, 6.0, ((1, 32),))
    new_values = bell_draw(arg_keys[8], (2, REQUESTS, ROWS, KVH * HD), 1.0, 6.0, ((1, 32),))
    norm_gain = jnp.clip(1.0 + 0.15 * jax.random.normal(arg_keys[9], (D,), jnp.float32), 0.25, 1.75)
    expert_ids_keys = jax.random.split(jax.random.fold_in(arg_keys[10], 1), 2 * REQUESTS * ROWS // ROWS)
    expert_ids_turns = jax.random.permutation(jax.random.fold_in(arg_keys[10], 3), 2 * REQUESTS * ROWS // ROWS)
    expert_ids = jax.vmap(lambda own, number: assign_block(jax.random.fold_in(arg_keys[10], 2), own, number, ROWS, EXPERTS, TOP, CAP, 2))(expert_ids_keys, expert_ids_turns).reshape((2, REQUESTS, ROWS, TOP))
    gate_weights = jnp.clip(0.049804688 + 0.3486328 * jax.random.uniform(arg_keys[11], (2, REQUESTS, ROWS, TOP), jnp.float32) ** level_of(arg_keys[11], (2, REQUESTS, ROWS, TOP), ((1, 32),), -0.2, 0.2), 0.049804688, 0.3984375).astype(jnp.bfloat16)
    w_gate = bell_draw(arg_keys[12], (EXPERTS, D, FFE), D ** -0.5, 0.09375, ((0, 16), (2, 2)))
    w_up = bell_draw(arg_keys[13], (EXPERTS, D, FFE), D ** -0.5, 0.09375, ((0, 16), (2, 2)))
    w_down = bell_draw(arg_keys[14], (EXPERTS, FFE, D), FFE ** -0.5, 0.1875, ((0, 16), (1, 2)))
    return dict(cache_keys=cache_keys, cache_values=cache_values, lengths=lengths, drift_rows=drift_rows, block_in=block_in, drift_in=drift_in, queries=queries, new_keys=new_keys, new_values=new_values, norm_gain=norm_gain, expert_ids=expert_ids, gate_weights=gate_weights, w_gate=w_gate, w_up=w_up, w_down=w_down)


def attend(query_rows, key_rows, value_rows, block_keys, block_values, length):
    row_count = query_rows.shape[0]
    group_size = H // KVH
    query_head_rows = query_rows.astype(jnp.float32).reshape(row_count, KVH, group_size, HD)
    cache_k = key_rows.astype(jnp.float32).reshape(-1, KVH, HD)
    cached_value_rows = value_rows.astype(jnp.float32).reshape(-1, KVH, HD)
    prompt_key_rows = block_keys.astype(jnp.float32).reshape(-1, KVH, HD)
    prompt_value_rows = block_values.astype(jnp.float32).reshape(-1, KVH, HD)
    logit_scale_factor = HD ** (-0.5)
    cache_scores = jnp.einsum('rkgd,ckd->kgrc', query_head_rows, cache_k) * logit_scale_factor
    prompt_score_rows = jnp.einsum('afhu,nfu->fhan', query_head_rows, prompt_key_rows) * logit_scale_factor
    cache_mask = jnp.arange(cache_k.shape[0]) < length
    own_mask = (jnp.arange(row_count) < BLOCK)[:, None]
    cache_scores = jnp.where(cache_mask, cache_scores, -1e+30)
    prompt_score_rows = jnp.where(own_mask, prompt_score_rows, -1e+30)
    peak = jnp.maximum(lax.optimization_barrier(jnp.max(cache_scores, axis=-1)), lax.optimization_barrier(jnp.max(prompt_score_rows, axis=-1)))
    cache_exp = jnp.exp(cache_scores - peak[..., None])
    own_exp = jnp.exp(prompt_score_rows - peak[..., None])
    denom = lax.optimization_barrier(jnp.sum(cache_exp, axis=-1)) + lax.optimization_barrier(jnp.sum(own_exp, axis=-1))
    cached_weight_share = (cache_exp / denom[..., None]).astype(jnp.bfloat16).astype(jnp.float32)
    prompt_weight_share = (own_exp / denom[..., None]).astype(jnp.bfloat16).astype(jnp.float32)
    blended_output = jnp.einsum('qimt,tqj->mqij', cached_weight_share, cached_value_rows) + jnp.einsum('iywf,fie->wiye', prompt_weight_share, prompt_value_rows)
    return blended_output.reshape(row_count, H * HD)

def route_table(routed, gate_share):
    member = routed[:, :, None] == jnp.arange(EXPERTS)[None, None, :]
    weight = lax.optimization_barrier(jnp.sum(jnp.where(member, gate_share[:, :, None].astype(jnp.float32), 0.0), axis=1))
    chosen = jnp.any(member, axis=1).astype(jnp.int32)
    slot_rank = jnp.cumsum(chosen, axis=0) - chosen
    taken = (slot_rank[:, :, None] == jnp.arange(CAP)[None, None, :]) & (chosen[:, :, None] == 1)
    return jnp.where(taken, weight[:, :, None], 0.0).astype(jnp.bfloat16)

def mixture(normed, tables, w_gate, w_up, w_down):
    quarter = FFE // N_REP

    def add_expert(running, expert):
        slot_table = lax.dynamic_index_in_dim(tables, expert, axis=2, keepdims=False)
        chosen = (slot_table != 0).astype(jnp.float32)
        dispatched = jnp.einsum('rjc,rjd->rcd', chosen, normed.astype(jnp.float32))
        flat_rows = dispatched.reshape(-1, D).astype(jnp.bfloat16)
        gate_act = jnp.dot(flat_rows, w_gate[expert], preferred_element_type=jnp.float32)
        up_act = jnp.dot(flat_rows, w_up[expert], preferred_element_type=jnp.float32)
        hidden = (jax.nn.silu(gate_act) * up_act).astype(jnp.bfloat16)
        down_rows = w_down[expert]
        summed = jnp.zeros((flat_rows.shape[0], D), jnp.float32)
        for index in range(N_REP):
            part_out = jnp.dot(hidden[:, index * quarter:(index + 1) * quarter], down_rows[index * quarter:(index + 1) * quarter], preferred_element_type=jnp.float32).astype(jnp.bfloat16)
            summed = summed + lax.optimization_barrier(part_out).astype(jnp.float32)
        summed = summed.reshape(REQUESTS, CAP, D)
        running = running + jnp.einsum('rjc,rcd->rjd', slot_table.astype(jnp.float32), summed)
        return (running, None)
    start = jnp.zeros((REQUESTS, ROWS, D), jnp.float32)
    running, _ = lax.scan(add_expert, start, jnp.arange(EXPERTS).astype(jnp.int32))
    return running

def reference(cache_keys, cache_values, lengths, drift_rows, block_in, drift_in, queries, new_keys, new_values, norm_gain, expert_ids, gate_weights, w_gate, w_up, w_down):
    outputs = []
    carried = block_in
    drift_by_req = jnp.swapaxes(drift_rows, 0, 1)
    query_by_req = jnp.swapaxes(queries, 0, 1)
    keys_by_req = jnp.swapaxes(new_keys, 0, 1)
    values_by_req = jnp.swapaxes(new_values, 0, 1)
    for denoise in range(2):

        def per_request(packed):
            key_rows, value_rows, length, drifts, query_rows, fresh_k, fresh_v = packed
            for past in range(denoise + 1):
                key_rows = key_rows.at[drifts[past]].set(fresh_k[past, BLOCK:])
                value_rows = value_rows.at[drifts[past]].set(fresh_v[past, BLOCK:])
            return attend(query_rows[denoise], key_rows, value_rows, fresh_k[denoise, :BLOCK], fresh_v[denoise, :BLOCK], length)
        attended = lax.map(per_request, (cache_keys, cache_values, lengths, drift_by_req, query_by_req, keys_by_req, values_by_req))
        inputs = jnp.concatenate([carried, drift_in[denoise]], axis=1).astype(jnp.float32)
        residual = inputs + attended
        inverse = lax.rsqrt(lax.optimization_barrier(jnp.mean(residual * residual, axis=-1, keepdims=True)) + 1e-06)
        normed = (residual * inverse * norm_gain).astype(jnp.bfloat16)
        tables = jax.vmap(route_table)(expert_ids[denoise], gate_weights[denoise])
        moe = mixture(normed, tables, w_gate, w_up, w_down)
        result = (residual + moe).astype(jnp.bfloat16)
        outputs.append(result)
        carried = result[:, :BLOCK]
    return jnp.stack(outputs)
```

```python
import jax
import jax.numpy as jnp
from jax import lax
from jax.experimental import pallas as pl
from jax.experimental.pallas import tpu as pltpu
from jax.sharding import PartitionSpec as P

H = 32
KVH = 4
HD = 128
TOP = 8
BLOCK = 8


def attend(query_rows, key_rows, value_rows, block_keys, block_values, length):
    row_count = query_rows.shape[0]
    group_size = H // KVH
    query_head_rows = query_rows.reshape(row_count, KVH, group_size, HD)
    cache_k = key_rows.reshape(-1, KVH, HD)
    cached_value_rows = value_rows.reshape(-1, KVH, HD)
    prompt_key_rows = block_keys.reshape(-1, KVH, HD)
    prompt_value_rows = block_values.reshape(-1, KVH, HD)
    logit_scale_factor = HD ** (-0.5)
    cache_scores = (
        jnp.einsum("rkgd,ckd->kgrc", query_head_rows, cache_k, preferred_element_type=jnp.float32)
        * logit_scale_factor
    )
    prompt_score_rows = (
        jnp.einsum(
            "afhu,nfu->fhan", query_head_rows, prompt_key_rows, preferred_element_type=jnp.float32
        )
        * logit_scale_factor
    )
    cache_mask = jnp.arange(cache_k.shape[0]) < length
    own_mask = (jnp.arange(row_count) < BLOCK)[:, None]
    cache_scores = jnp.where(cache_mask, cache_scores, -1e30)
    prompt_score_rows = jnp.where(own_mask, prompt_score_rows, -1e30)
    peak = jnp.maximum(jnp.max(cache_scores, axis=-1), jnp.max(prompt_score_rows, axis=-1))
    cache_exp = jnp.exp(cache_scores - peak[..., None])
    own_exp = jnp.exp(prompt_score_rows - peak[..., None])
    denom = jnp.sum(cache_exp, axis=-1) + jnp.sum(own_exp, axis=-1)
    cached_weight_share = (cache_exp / denom[..., None]).astype(jnp.bfloat16)
    prompt_weight_share = (own_exp / denom[..., None]).astype(jnp.bfloat16)
    blended_output = jnp.einsum(
        "qimt,tqj->mqij", cached_weight_share, cached_value_rows, preferred_element_type=jnp.float32
    )
    blended_output = blended_output + jnp.einsum(
        "iywf,fie->wiye", prompt_weight_share, prompt_value_rows, preferred_element_type=jnp.float32
    )
    return blended_output.reshape(row_count, H * HD)


def route_table(routed, gate_share, experts, capacity):
    member = routed[:, :, None] == jnp.arange(experts)[None, None, :]
    weight = jnp.sum(jnp.where(member, gate_share[:, :, None].astype(jnp.float32), 0.0), axis=1)
    chosen = jnp.any(member, axis=1).astype(jnp.int32)
    slot_rank = jnp.cumsum(chosen, axis=0) - chosen
    taken = (slot_rank[:, :, None] == jnp.arange(capacity)[None, None, :]) & (
        chosen[:, :, None] == 1
    )
    return jnp.where(taken, weight[:, :, None], 0.0).astype(jnp.bfloat16)


def expert_terms(routed_rows, gate_part, up_part, down_part):
    flat_rows = routed_rows.reshape(-1, routed_rows.shape[-1])
    gate_act = jnp.dot(flat_rows, gate_part, preferred_element_type=jnp.float32)
    up_act = jnp.dot(flat_rows, up_part, preferred_element_type=jnp.float32)
    hidden = (jax.nn.silu(gate_act) * up_act).astype(jnp.bfloat16)
    produced = jnp.dot(hidden, down_part, preferred_element_type=jnp.float32).astype(jnp.bfloat16)
    return produced.reshape(routed_rows.shape)


def on_device(
    cache_keys,
    cache_values,
    lengths,
    drift_rows,
    block_in,
    drift_in,
    queries,
    new_keys,
    new_values,
    norm_gain,
    expert_ids,
    gate_weights,
    w_gate,
    w_up,
    w_down,
):
    rep_count = lax.axis_size("rep")
    experts = lax.axis_size("exp") * w_gate.shape[0]
    row_count = queries.shape[2]
    capacity = min(row_count, (3 * row_count * TOP + 2 * experts - 1) // (2 * experts))
    key_rows = cache_keys[0]
    value_rows = cache_values[0]
    carried = block_in[0]
    results = []
    for denoise in range(2):
        key_rows = key_rows.at[drift_rows[denoise, 0]].set(new_keys[denoise, 0, BLOCK:])
        value_rows = value_rows.at[drift_rows[denoise, 0]].set(new_values[denoise, 0, BLOCK:])
        attended = attend(
            queries[denoise, 0],
            key_rows,
            value_rows,
            new_keys[denoise, 0, :BLOCK],
            new_values[denoise, 0, :BLOCK],
            lengths[0],
        )
        inputs = jnp.concatenate([carried, drift_in[denoise, 0]], axis=0).astype(jnp.float32)
        residual = inputs + attended
        inverse = lax.rsqrt(jnp.mean(residual * residual, axis=-1, keepdims=True) + 1e-06)
        normed = (residual * inverse * norm_gain).astype(jnp.bfloat16)
        slot_table = route_table(
            expert_ids[denoise, 0], gate_weights[denoise, 0], experts, capacity
        )
        flat_table = slot_table.reshape(row_count, experts * capacity)
        all_rows, all_tables = (
            lax.all_gather(normed, "rep", axis=0, tiled=True),
            lax.all_gather(flat_table, "rep", axis=0, tiled=True),
        )
        all_rows = all_rows.reshape(rep_count, row_count, -1)
        all_tables = all_tables.reshape(rep_count, row_count, experts, capacity)
        chosen_slots = (all_tables != 0).astype(jnp.bfloat16)
        dispatched = jnp.einsum(
            "orec,ord->eocd", chosen_slots, all_rows, preferred_element_type=jnp.float32
        ).astype(jnp.bfloat16)
        produced = expert_terms(
            lax.all_to_all(dispatched, "exp", split_axis=0, concat_axis=0, tiled=True),
            w_gate[0],
            w_up[0],
            w_down[0],
        )
        expert_out = lax.all_to_all(produced, "exp", split_axis=0, concat_axis=0, tiled=True)
        combined = jnp.einsum(
            "orec,eocd->ord", all_tables, expert_out, preferred_element_type=jnp.float32
        )
        moe = lax.psum_scatter(
            combined.reshape(rep_count * row_count, -1).astype(jnp.bfloat16),
            "rep",
            scatter_dimension=0,
            tiled=True,
        ).astype(jnp.float32)
        result = (residual + moe).astype(jnp.bfloat16)
        results.append(result)
        carried = result[:BLOCK]
    return jnp.stack(results)[:, None]


GROUP = H // KVH
EXTRA = 128


def attention_kernel(q_ref, k_ref, v_ref, xk_ref, xv_ref, mask_ref, xmask_ref, out_ref):
    scale = HD ** (-0.5)
    keys, values = k_ref[...], v_ref[...]
    row_count = q_ref.shape[1]
    for step in range(2):
        q = jnp.concatenate(
            [q_ref[step, :, g * HD : (g + 1) * HD] for g in range(GROUP)], axis=0
        )
        nt = (((1,), (1,)), ((), ()))
        scores = lax.dot_general(q, keys, nt, preferred_element_type=jnp.float32)
        scores = scores * scale + mask_ref[step]
        extra = lax.dot_general(q, xk_ref[step], nt, preferred_element_type=jnp.float32)
        extra = extra * scale + xmask_ref[step]
        peak = jnp.maximum(
            jnp.max(scores, axis=1, keepdims=True), jnp.max(extra, axis=1, keepdims=True)
        )
        scores = jnp.exp(scores - peak)
        extra = jnp.exp(extra - peak)
        denom = jnp.sum(scores, axis=1, keepdims=True) + jnp.sum(extra, axis=1, keepdims=True)
        mixed = jnp.dot(scores.astype(jnp.bfloat16), values, preferred_element_type=jnp.float32)
        mixed += jnp.dot(
            extra.astype(jnp.bfloat16), xv_ref[step], preferred_element_type=jnp.float32
        )
        mixed = mixed / denom
        for g in range(GROUP):
            out_ref[step, :, g * HD : (g + 1) * HD] = mixed[g * row_count : (g + 1) * row_count]


def attend_both(keys, values, length, drift, queries, new_keys, new_values):
    row_count, slots = queries.shape[1], keys.shape[0]
    places = jnp.arange(slots)
    hit = jnp.any(places[None, None, :] == drift[:, :, None], axis=1)
    valid = places < length
    open_ = jnp.stack([valid & ~hit[0], valid & ~hit[0] & ~hit[1]])
    mask = jnp.where(open_, 0.0, -1e30).astype(jnp.float32)[:, None, :]
    kept = ~jnp.any(drift[0][:, None] == drift[1][None, :], axis=1)
    own = (jnp.arange(row_count) < BLOCK)[None, :, None]
    own = jnp.broadcast_to(own, (2, row_count, BLOCK))
    fresh = jnp.ones((2, row_count, row_count - BLOCK), bool)
    older = jnp.stack([jnp.zeros_like(kept), kept])[:, None, :]
    older = jnp.broadcast_to(older, (2, row_count, kept.shape[0]))
    rest = jnp.zeros((2, row_count, EXTRA - row_count - kept.shape[0]), bool)
    xmask = jnp.where(jnp.concatenate([own, fresh, older, rest], axis=2), 0.0, -1e30)
    xmask = jnp.tile(xmask.astype(jnp.float32), (1, GROUP, 1))

    def extras(new):
        again = jnp.broadcast_to(new[:1, BLOCK:], (2, row_count - BLOCK, new.shape[2]))
        joined = jnp.concatenate([new, again], axis=1)
        return jnp.pad(joined, ((0, 0), (0, EXTRA - joined.shape[1]), (0, 0)))

    wide = GROUP * HD
    return pl.pallas_call(
        attention_kernel,
        grid=(KVH,),
        in_specs=[
            pl.BlockSpec((2, row_count, wide), lambda j: (0, 0, j)),
            pl.BlockSpec((slots, HD), lambda j: (0, j)),
            pl.BlockSpec((slots, HD), lambda j: (0, j)),
            pl.BlockSpec((2, EXTRA, HD), lambda j: (0, 0, j)),
            pl.BlockSpec((2, EXTRA, HD), lambda j: (0, 0, j)),
            pl.BlockSpec((2, 1, slots), lambda j: (0, 0, 0)),
            pl.BlockSpec((2, GROUP * row_count, EXTRA), lambda j: (0, 0, 0)),
        ],
        out_specs=pl.BlockSpec((2, row_count, wide), lambda j: (0, 0, j)),
        out_shape=jax.ShapeDtypeStruct((2, row_count, H * HD), jnp.float32),
        compiler_params=pltpu.CompilerParams(vmem_limit_bytes=40 * 2**20),
        name="attention",
    )(queries, keys, values, extras(new_keys), extras(new_values), mask, xmask)


def swapped(i):
    return (i // 4 % 2) * 8 + (i // 8) * 4 + i % 4


SLOTS = 32


def expert_kernel(
    base, tables, gain, wg_in, wu_in, wd_in, out,
    rows, part, hidden, from_core, from_b, from_a, from_z, residual, carried, wg, wu, wd,
    w_sem, ag_send, ag_recv, rs_send, rs_recv,
):
    y, e = lax.axis_index("rep"), lax.axis_index("exp")
    c, x, z = lax.rem(e, 2), lax.rem(lax.div(e, 2), 2), lax.div(e, 4)
    z_low, z_high = lax.rem(z, 2), lax.div(z, 2)

    def device(y_, z_, x_, c_):
        return (y_, (z_ * 2 + x_) * 2 + c_)

    core = device(y, z, x, 1 - c)
    a_side = device(y + c * (1 - 2 * y), z, x + (1 - c) * (1 - 2 * x), c)
    b_side = device(y + (1 - c) * (1 - 2 * y), z, x + c * (1 - 2 * x), c)
    z_side = [None] + [
        device(
            y,
            ((1 - z_high) if k & 2 else z_high) * 2 + ((1 - z_low) if k & 1 else z_low),
            x,
            c,
        )
        for k in (1, 2, 3)
    ]

    loads = [
        pltpu.make_async_copy(src, dst, w_sem.at[i])
        for i, (src, dst) in enumerate(((wg_in, wg), (wu_in, wu), (wd_in, wd)))
    ]
    for load in loads:
        load.start()

    barrier = pltpu.get_barrier_semaphore()
    for peer in (core, a_side, b_side, *z_side[1:]):
        pl.semaphore_signal(barrier, inc=1, device_id=peer, device_id_type=pl.DeviceIdType.MESH)
    pl.semaphore_wait(barrier, 6)

    def remote(src, dst, send, recv, peer):
        return pltpu.make_async_remote_copy(
            src_ref=src,
            dst_ref=dst,
            send_sem=send,
            recv_sem=recv,
            device_id=peer,
            device_id_type=pl.DeviceIdType.MESH,
        )

    def gather_copy(d):
        if d < 4:
            src, peer = 0, z_side[d]
        elif d < 8:
            src, peer = d - 4, a_side
        elif d < 16:
            src, peer = d - 8, b_side
        else:
            src, peer = swapped(d - 16), core
        return remote(rows.at[src], rows.at[d], ag_send.at[d], ag_recv.at[d], peer)

    def core_copy(j):
        return remote(
            part.at[16 + swapped(j)], from_core.at[j], rs_send.at[j], rs_recv.at[j], core
        )

    def b_copy(j):
        return remote(
            part.at[8 + j], from_b.at[j], rs_send.at[16 + j], rs_recv.at[16 + j], b_side
        )

    def a_copy(j):
        return remote(
            part.at[4 + j], from_a.at[j], rs_send.at[24 + j], rs_recv.at[24 + j], a_side
        )

    def z_copy(k):
        return remote(
            part.at[k], from_z.at[k], rs_send.at[28 + k], rs_recv.at[28 + k], z_side[k]
        )

    width = wd.shape[1]
    tile = 256
    row_count = rows.shape[1]
    half = 16 * row_count

    def experts(which):
        span = pl.ds(which * 16, 16)
        share = rows[span, :, width:].reshape(half, rows.shape[2] - width).astype(jnp.float32)
        lane = lax.broadcasted_iota(jnp.int32, share.shape, 1)
        share = jnp.sum(jnp.where(lane == e, share, 0.0), axis=1, keepdims=True)

        def up_tile(n, _):
            columns = pl.ds(pl.multiple_of(n * tile, tile), tile)
            x_rows = rows[span, :, :width].reshape(half, width)
            gate = jnp.dot(x_rows, wg[:, columns], preferred_element_type=jnp.float32)
            up = jnp.dot(x_rows, wu[:, columns], preferred_element_type=jnp.float32)
            act = gate / (1.0 + jnp.exp(-gate)) * up * share
            hidden[:, columns] = act.astype(jnp.bfloat16)
            return 0

        lax.fori_loop(0, hidden.shape[1] // tile, up_tile, 0)

        def down_tile(n, _):
            columns = pl.ds(pl.multiple_of(n * tile, tile), tile)
            made = jnp.dot(hidden[...], wd[:, columns], preferred_element_type=jnp.float32)
            part[span, :, columns] = made.astype(jnp.bfloat16).reshape(16, row_count, tile)
            return 0

        lax.fori_loop(0, width // tile, down_tile, 0)

    carried[...] = jnp.zeros_like(carried)

    def one_step(step, _):
        residual[...] = base[step]
        residual[:BLOCK] = residual[:BLOCK] + carried[...]
        held = residual[...]
        inverse = lax.rsqrt(jnp.mean(held * held, axis=1, keepdims=True) + 1e-06)
        rows[0, :, :width] = (held * inverse * gain[...]).astype(jnp.bfloat16)
        rows[0, :, width:] = tables[step]

        for d in (1, 2, 3, 4, 8, 16):
            gather_copy(d).start()
        for d in (1, 4, 2, 8, 3, 5, 9, 6, 10, 7, 11, 12, 13, 14, 15):
            gather_copy(d).wait_recv()
            if d < 4:
                gather_copy(4 + d).start()
            if d < 8:
                gather_copy(8 + d).start()
            gather_copy(16 + swapped(d)).start()
        for d in range(16, SLOTS):
            gather_copy(d).wait_recv()
        for d in range(1, SLOTS):
            gather_copy(d).wait_send()

        @pl.when(step == 0)
        def _():
            for load in loads:
                load.wait()

        experts(1)
        order = (12, 13, 14, 15, 8, 9, 10, 11, 4, 5, 6, 7, 1, 2, 3, 0)
        for j in order:
            core_copy(j).start()
        experts(0)
        for j in order:
            core_copy(j).wait_recv()
            total = part[j].astype(jnp.float32) + from_core[j].astype(jnp.float32)
            if j < 8:
                b_copy(j).wait_recv()
                total = total + from_b[j].astype(jnp.float32)
            if j < 4:
                a_copy(j).wait_recv()
                total = total + from_a[j].astype(jnp.float32)
            if j > 0:
                part[j] = total.astype(jnp.bfloat16)
                (b_copy(j - 8) if j >= 8 else a_copy(j - 4) if j >= 4 else z_copy(j)).start()
            else:
                for k in (1, 2, 3):
                    z_copy(k).wait_recv()
                    total = total + from_z[k].astype(jnp.float32)
                result = (residual[...] + total).astype(jnp.bfloat16)
                out[step] = result
                carried[...] = result.astype(jnp.float32)[:BLOCK]
        for j in range(16):
            core_copy(j).wait_send()
        for j in range(8):
            b_copy(j).wait_send()
        for j in range(4):
            a_copy(j).wait_send()
        for k in (1, 2, 3):
            z_copy(k).wait_send()
        return 0

    lax.fori_loop(0, 2, one_step, 0)


def on_device_close(
    cache_keys, cache_values, lengths, drift_rows, block_in, drift_in, queries, new_keys,
    new_values, norm_gain, expert_ids, gate_weights, w_gate, w_up, w_down,
):
    attended = attend_both(
        cache_keys[0],
        cache_values[0],
        lengths[0],
        drift_rows[:, 0],
        queries[:, 0],
        new_keys[:, 0],
        new_values[:, 0],
    )
    row_count, width = queries.shape[2], queries.shape[3]
    first = jnp.stack([block_in[0], jnp.zeros_like(block_in[0])])
    base = attended + jnp.concatenate([first, drift_in[:, 0]], axis=1).astype(jnp.float32)
    member = expert_ids[:, 0, :, :, None] == jnp.arange(128)
    tables = jnp.sum(jnp.where(member, gate_weights[:, 0, :, :, None], 0), axis=2)
    tables = tables.astype(jnp.bfloat16)
    vmem = pl.BlockSpec(memory_space=pltpu.VMEM)
    hbm = pl.BlockSpec(memory_space=pl.ANY)
    block = (row_count, width)
    bf16 = jnp.bfloat16
    out = pl.pallas_call(
        expert_kernel,
        out_shape=jax.ShapeDtypeStruct((2, row_count, width), bf16),
        in_specs=[vmem, vmem, vmem, hbm, hbm, hbm],
        out_specs=vmem,
        scratch_shapes=[
            pltpu.VMEM((SLOTS, row_count, width + 128), bf16),
            pltpu.VMEM((SLOTS, *block), bf16),
            pltpu.VMEM((16 * row_count, w_down.shape[1]), bf16),
            pltpu.VMEM((16, *block), bf16),
            pltpu.VMEM((8, *block), bf16),
            pltpu.VMEM((4, *block), bf16),
            pltpu.VMEM((4, *block), bf16),
            pltpu.VMEM(block, jnp.float32),
            pltpu.VMEM((BLOCK, width), jnp.float32),
            pltpu.VMEM(w_gate.shape[1:], bf16),
            pltpu.VMEM(w_up.shape[1:], bf16),
            pltpu.VMEM(w_down.shape[1:], bf16),
            pltpu.SemaphoreType.DMA((3,)),
            pltpu.SemaphoreType.DMA((SLOTS,)),
            pltpu.SemaphoreType.DMA((SLOTS,)),
            pltpu.SemaphoreType.DMA((SLOTS,)),
            pltpu.SemaphoreType.DMA((SLOTS,)),
        ],
        compiler_params=pltpu.CompilerParams(
            collective_id=0, has_side_effects=True, vmem_limit_bytes=48 * 2**20
        ),
        name="experts",
    )(base, tables, norm_gain[None], w_gate[0], w_up[0], w_down[0])
    return out[:, None]


def solution(mesh):
    close = mesh.shape["rep"] == 2 and mesh.shape["exp"] == 16
    placed = (
        P(("rep", "exp"), None, None),
        P(("rep", "exp"), None, None),
        P(("rep", "exp")),
        P(None, ("rep", "exp"), None),
        P(("rep", "exp"), None, None),
        P(None, ("rep", "exp"), None, None),
        P(None, ("rep", "exp"), None, None),
        P(None, ("rep", "exp"), None, None),
        P(None, ("rep", "exp"), None, None),
        P(),
        P(None, ("rep", "exp"), None, None),
        P(None, ("rep", "exp"), None, None),
        P("exp", None, "rep"),
        P("exp", None, "rep"),
        P("exp", "rep", None),
    )
    return jax.shard_map(
        on_device_close if close else on_device,
        mesh=mesh,
        in_specs=placed,
        out_specs=P(None, ("rep", "exp"), None, None),
        check_vma=False,
    )
```

```python
import jax
import jax.numpy as jnp
from jax import lax
from jax.experimental import pallas as pl
from jax.experimental.pallas import tpu as pltpu
from jax.sharding import PartitionSpec as P

H = 32
KVH = 4
HD = 128
TOP = 8
BLOCK = 8


def attend(query_rows, key_rows, value_rows, block_keys, block_values, length):
    row_count = query_rows.shape[0]
    group_size = H // KVH
    query_head_rows = query_rows.reshape(row_count, KVH, group_size, HD)
    cache_k = key_rows.reshape(-1, KVH, HD)
    cached_value_rows = value_rows.reshape(-1, KVH, HD)
    prompt_key_rows = block_keys.reshape(-1, KVH, HD)
    prompt_value_rows = block_values.reshape(-1, KVH, HD)
    logit_scale_factor = HD ** (-0.5)
    cache_scores = (
        jnp.einsum("rkgd,ckd->kgrc", query_head_rows, cache_k, preferred_element_type=jnp.float32)
        * logit_scale_factor
    )
    prompt_score_rows = (
        jnp.einsum(
            "afhu,nfu->fhan", query_head_rows, prompt_key_rows, preferred_element_type=jnp.float32
        )
        * logit_scale_factor
    )
    cache_mask = jnp.arange(cache_k.shape[0]) < length
    own_mask = (jnp.arange(row_count) < BLOCK)[:, None]
    cache_scores = jnp.where(cache_mask, cache_scores, -1e30)
    prompt_score_rows = jnp.where(own_mask, prompt_score_rows, -1e30)
    peak = jnp.maximum(jnp.max(cache_scores, axis=-1), jnp.max(prompt_score_rows, axis=-1))
    cache_exp = jnp.exp(cache_scores - peak[..., None])
    own_exp = jnp.exp(prompt_score_rows - peak[..., None])
    denom = jnp.sum(cache_exp, axis=-1) + jnp.sum(own_exp, axis=-1)
    cached_weight_share = (cache_exp / denom[..., None]).astype(jnp.bfloat16)
    prompt_weight_share = (own_exp / denom[..., None]).astype(jnp.bfloat16)
    blended_output = jnp.einsum(
        "qimt,tqj->mqij", cached_weight_share, cached_value_rows, preferred_element_type=jnp.float32
    )
    blended_output = blended_output + jnp.einsum(
        "iywf,fie->wiye", prompt_weight_share, prompt_value_rows, preferred_element_type=jnp.float32
    )
    return blended_output.reshape(row_count, H * HD)


def route_table(routed, gate_share, experts, capacity):
    member = routed[:, :, None] == jnp.arange(experts)[None, None, :]
    weight = jnp.sum(jnp.where(member, gate_share[:, :, None].astype(jnp.float32), 0.0), axis=1)
    chosen = jnp.any(member, axis=1).astype(jnp.int32)
    slot_rank = jnp.cumsum(chosen, axis=0) - chosen
    taken = (slot_rank[:, :, None] == jnp.arange(capacity)[None, None, :]) & (
        chosen[:, :, None] == 1
    )
    return jnp.where(taken, weight[:, :, None], 0.0).astype(jnp.bfloat16)


def expert_terms(routed_rows, gate_part, up_part, down_part):
    flat_rows = routed_rows.reshape(-1, routed_rows.shape[-1])
    gate_act = jnp.dot(flat_rows, gate_part, preferred_element_type=jnp.float32)
    up_act = jnp.dot(flat_rows, up_part, preferred_element_type=jnp.float32)
    hidden = (jax.nn.silu(gate_act) * up_act).astype(jnp.bfloat16)
    produced = jnp.dot(hidden, down_part, preferred_element_type=jnp.float32).astype(jnp.bfloat16)
    return produced.reshape(routed_rows.shape)


def on_device(
    cache_keys,
    cache_values,
    lengths,
    drift_rows,
    block_in,
    drift_in,
    queries,
    new_keys,
    new_values,
    norm_gain,
    expert_ids,
    gate_weights,
    w_gate,
    w_up,
    w_down,
):
    rep_count = lax.axis_size("rep")
    experts = lax.axis_size("exp") * w_gate.shape[0]
    row_count = queries.shape[2]
    capacity = min(row_count, (3 * row_count * TOP + 2 * experts - 1) // (2 * experts))
    key_rows = cache_keys[0]
    value_rows = cache_values[0]
    carried = block_in[0]
    results = []
    for denoise in range(2):
        key_rows = key_rows.at[drift_rows[denoise, 0]].set(new_keys[denoise, 0, BLOCK:])
        value_rows = value_rows.at[drift_rows[denoise, 0]].set(new_values[denoise, 0, BLOCK:])
        attended = attend(
            queries[denoise, 0],
            key_rows,
            value_rows,
            new_keys[denoise, 0, :BLOCK],
            new_values[denoise, 0, :BLOCK],
            lengths[0],
        )
        inputs = jnp.concatenate([carried, drift_in[denoise, 0]], axis=0).astype(jnp.float32)
        residual = inputs + attended
        inverse = lax.rsqrt(jnp.mean(residual * residual, axis=-1, keepdims=True) + 1e-06)
        normed = (residual * inverse * norm_gain).astype(jnp.bfloat16)
        slot_table = route_table(
            expert_ids[denoise, 0], gate_weights[denoise, 0], experts, capacity
        )
        flat_table = slot_table.reshape(row_count, experts * capacity)
        all_rows, all_tables = (
            lax.all_gather(normed, "rep", axis=0, tiled=True),
            lax.all_gather(flat_table, "rep", axis=0, tiled=True),
        )
        all_rows = all_rows.reshape(rep_count, row_count, -1)
        all_tables = all_tables.reshape(rep_count, row_count, experts, capacity)
        chosen_slots = (all_tables != 0).astype(jnp.bfloat16)
        dispatched = jnp.einsum(
            "orec,ord->eocd", chosen_slots, all_rows, preferred_element_type=jnp.float32
        ).astype(jnp.bfloat16)
        produced = expert_terms(
            lax.all_to_all(dispatched, "exp", split_axis=0, concat_axis=0, tiled=True),
            w_gate[0],
            w_up[0],
            w_down[0],
        )
        expert_out = lax.all_to_all(produced, "exp", split_axis=0, concat_axis=0, tiled=True)
        combined = jnp.einsum(
            "orec,eocd->ord", all_tables, expert_out, preferred_element_type=jnp.float32
        )
        moe = lax.psum_scatter(
            combined.reshape(rep_count * row_count, -1).astype(jnp.bfloat16),
            "rep",
            scatter_dimension=0,
            tiled=True,
        ).astype(jnp.float32)
        result = (residual + moe).astype(jnp.bfloat16)
        results.append(result)
        carried = result[:BLOCK]
    return jnp.stack(results)[:, None]


GROUP = H // KVH
EXTRA = 128


def attention_kernel(q_ref, k_ref, v_ref, xk_ref, xv_ref, mask_ref, xmask_ref, out_ref):
    scale = HD ** (-0.5)
    keys, values = k_ref[...], v_ref[...]
    row_count = q_ref.shape[1]
    for step in range(2):
        q = jnp.concatenate(
            [q_ref[step, :, g * HD : (g + 1) * HD] for g in range(GROUP)], axis=0
        )
        nt = (((1,), (1,)), ((), ()))
        scores = lax.dot_general(q, keys, nt, preferred_element_type=jnp.float32)
        scores = scores * scale + mask_ref[step]
        extra = lax.dot_general(q, xk_ref[step], nt, preferred_element_type=jnp.float32)
        extra = extra * scale + xmask_ref[step]
        peak = jnp.maximum(
            jnp.max(scores, axis=1, keepdims=True), jnp.max(extra, axis=1, keepdims=True)
        )
        scores = jnp.exp(scores - peak)
        extra = jnp.exp(extra - peak)
        denom = jnp.sum(scores, axis=1, keepdims=True) + jnp.sum(extra, axis=1, keepdims=True)
        mixed = jnp.dot(scores.astype(jnp.bfloat16), values, preferred_element_type=jnp.float32)
        mixed += jnp.dot(
            extra.astype(jnp.bfloat16), xv_ref[step], preferred_element_type=jnp.float32
        )
        mixed = mixed / denom
        for g in range(GROUP):
            out_ref[step, :, g * HD : (g + 1) * HD] = mixed[g * row_count : (g + 1) * row_count]


def attend_both(keys, values, length, drift, queries, new_keys, new_values):
    row_count, slots = queries.shape[1], keys.shape[0]
    places = jnp.arange(slots)
    hit = jnp.any(places[None, None, :] == drift[:, :, None], axis=1)
    valid = places < length
    open_ = jnp.stack([valid & ~hit[0], valid & ~hit[0] & ~hit[1]])
    mask = jnp.where(open_, 0.0, -1e30).astype(jnp.float32)[:, None, :]
    kept = ~jnp.any(drift[0][:, None] == drift[1][None, :], axis=1)
    own = (jnp.arange(row_count) < BLOCK)[None, :, None]
    own = jnp.broadcast_to(own, (2, row_count, BLOCK))
    fresh = jnp.ones((2, row_count, row_count - BLOCK), bool)
    older = jnp.stack([jnp.zeros_like(kept), kept])[:, None, :]
    older = jnp.broadcast_to(older, (2, row_count, kept.shape[0]))
    rest = jnp.zeros((2, row_count, EXTRA - row_count - kept.shape[0]), bool)
    xmask = jnp.where(jnp.concatenate([own, fresh, older, rest], axis=2), 0.0, -1e30)
    xmask = jnp.tile(xmask.astype(jnp.float32), (1, GROUP, 1))

    def extras(new):
        again = jnp.broadcast_to(new[:1, BLOCK:], (2, row_count - BLOCK, new.shape[2]))
        joined = jnp.concatenate([new, again], axis=1)
        return jnp.pad(joined, ((0, 0), (0, EXTRA - joined.shape[1]), (0, 0)))

    wide = GROUP * HD
    return pl.pallas_call(
        attention_kernel,
        grid=(KVH,),
        in_specs=[
            pl.BlockSpec((2, row_count, wide), lambda j: (0, 0, j)),
            pl.BlockSpec((slots, HD), lambda j: (0, j)),
            pl.BlockSpec((slots, HD), lambda j: (0, j)),
            pl.BlockSpec((2, EXTRA, HD), lambda j: (0, 0, j)),
            pl.BlockSpec((2, EXTRA, HD), lambda j: (0, 0, j)),
            pl.BlockSpec((2, 1, slots), lambda j: (0, 0, 0)),
            pl.BlockSpec((2, GROUP * row_count, EXTRA), lambda j: (0, 0, 0)),
        ],
        out_specs=pl.BlockSpec((2, row_count, wide), lambda j: (0, 0, j)),
        out_shape=jax.ShapeDtypeStruct((2, row_count, H * HD), jnp.float32),
        compiler_params=pltpu.CompilerParams(vmem_limit_bytes=60 * 2**20),
        name="attention",
    )(queries, keys, values, extras(new_keys), extras(new_values), mask, xmask)


SLOTS = 32


def expert_kernel(
    base, tables, gain, wg_in, wu_in, wd_in, out,
    rows, part, hidden, from_core, from_b, from_a, from_z, residual, carried, wg, wu, wd,
    w_sem, ag_send, ag_recv, rs_send, rs_recv,
):
    y, e = lax.axis_index("rep"), lax.axis_index("exp")
    c, x, z = lax.rem(e, 2), lax.rem(lax.div(e, 2), 2), lax.div(e, 4)
    z_low, z_high = lax.rem(z, 2), lax.div(z, 2)

    def device(y_, z_, x_, c_):
        return (y_, (z_ * 2 + x_) * 2 + c_)

    core = device(y, z, x, 1 - c)
    a_side = device(y + c * (1 - 2 * y), z, x + (1 - c) * (1 - 2 * x), c)
    b_side = device(y + (1 - c) * (1 - 2 * y), z, x + c * (1 - 2 * x), c)
    z_side = [None] + [
        device(
            y,
            ((1 - z_high) if k & 2 else z_high) * 2 + ((1 - z_low) if k & 1 else z_low),
            x,
            c,
        )
        for k in (1, 2, 3)
    ]

    loads = [
        pltpu.make_async_copy(src, dst, w_sem.at[i])
        for i, (src, dst) in enumerate(((wg_in, wg), (wu_in, wu), (wd_in, wd)))
    ]
    for load in loads:
        load.start()

    barrier = pltpu.get_barrier_semaphore()
    for peer in (core, a_side, b_side, *z_side[1:]):
        pl.semaphore_signal(barrier, inc=1, device_id=peer, device_id_type=pl.DeviceIdType.MESH)
    pl.semaphore_wait(barrier, 6)

    def remote(src, dst, send, recv, peer):
        return pltpu.make_async_remote_copy(
            src_ref=src,
            dst_ref=dst,
            send_sem=send,
            recv_sem=recv,
            device_id=peer,
            device_id_type=pl.DeviceIdType.MESH,
        )

    def gather_copy(d):
        if d < 4:
            src, peer = 0, z_side[d]
        elif d < 8:
            src, peer = d - 4, a_side
        elif d < 16 or d >= 24:
            src, peer = d - 8, core
        else:
            src, peer = d - 16, b_side
        return remote(rows.at[src], rows.at[d], ag_send.at[d], ag_recv.at[d], peer)

    def core_copy(j):
        src = 8 + j if j < 8 else 16 + j
        return remote(part.at[src], from_core.at[j], rs_send.at[j], rs_recv.at[j], core)

    def b_copy(j):
        return remote(
            part.at[16 + j], from_b.at[j], rs_send.at[16 + j], rs_recv.at[16 + j], b_side
        )

    def a_copy(j):
        return remote(
            part.at[4 + j], from_a.at[j], rs_send.at[24 + j], rs_recv.at[24 + j], a_side
        )

    def z_copy(k):
        return remote(
            part.at[k], from_z.at[k], rs_send.at[28 + k], rs_recv.at[28 + k], z_side[k]
        )

    width = wd.shape[1]
    tile = 256
    row_count = rows.shape[1]
    half = 16 * row_count

    def up_tile(first, n):
        span = pl.ds(first, 16)
        share = rows[span, :, width:].reshape(half, rows.shape[2] - width).astype(jnp.float32)
        lane = lax.broadcasted_iota(jnp.int32, share.shape, 1)
        share = jnp.sum(jnp.where(lane == e, share, 0.0), axis=1, keepdims=True)
        columns = pl.ds(n * tile, tile)
        x_rows = rows[span, :, :width].reshape(half, width)
        gate = jnp.dot(x_rows, wg[:, columns], preferred_element_type=jnp.float32)
        up = jnp.dot(x_rows, wu[:, columns], preferred_element_type=jnp.float32)
        act = gate / (1.0 + jnp.exp(-gate)) * up * share
        hidden[:, columns] = act.astype(jnp.bfloat16)

    def down(first, offset):
        span = pl.ds(first, 8)

        def down_tile(n, _):
            columns = pl.ds(pl.multiple_of(n * 512, 512), 512)
            made = jnp.dot(
                hidden[pl.ds(offset, half // 2)],
                wd[:, columns],
                preferred_element_type=jnp.float32,
            )
            part[span, :, columns] = made.astype(jnp.bfloat16).reshape(8, row_count, 512)
            return 0

        lax.fori_loop(0, width // 512, down_tile, 0)

    carried[...] = jnp.zeros_like(carried)

    def one_step(step, _):
        residual[...] = base[step]
        residual[:BLOCK] = residual[:BLOCK] + carried[...]
        held = residual[...]
        inverse = lax.rsqrt(jnp.mean(held * held, axis=1, keepdims=True) + 1e-06)
        rows[0, :, :width] = (held * inverse * gain[...]).astype(jnp.bfloat16)
        rows[0, :, width:] = tables[step]

        for d in (16, 4, 1, 2, 3, 8):
            gather_copy(d).start()
        for d in (1, 4, 2, 3, 5, 6, 7):
            gather_copy(d).wait_recv()
            gather_copy(16 + d).start()
            if d < 4:
                gather_copy(4 + d).start()
            gather_copy(8 + d).start()

        def pass_on(*slots):
            for d in slots:
                gather_copy(d).wait_recv()
                gather_copy(8 + d).start()

        @pl.when(step == 0)
        def _():
            for load in loads:
                load.wait()

        for d in range(8, 16):
            gather_copy(d).wait_recv()
        up_tile(0, 0)
        pass_on(16, 17)
        up_tile(0, 1)
        pass_on(18, 20)
        down(8, half // 2)
        for j in range(8):
            core_copy(j).start()
        pass_on(19, 21)
        down(0, 0)
        pass_on(22, 23)
        for d in range(24, SLOTS):
            gather_copy(d).wait_recv()
        up_tile(16, 0)
        up_tile(16, 1)
        for d in range(1, SLOTS):
            gather_copy(d).wait_send()
        down(24, half // 2)
        far = (12, 13, 14, 15, 8, 9, 10, 11)
        for j in far:
            core_copy(j).start()
        down(16, 0)
        for j in (*far, 4, 5, 6, 7, 1, 2, 3, 0):
            mine = j if j < 8 else 8 + j
            core_copy(j).wait_recv()
            total = part[mine].astype(jnp.float32) + from_core[j].astype(jnp.float32)
            if j < 8:
                b_copy(j).wait_recv()
                total = total + from_b[j].astype(jnp.float32)
            if j < 4:
                a_copy(j).wait_recv()
                total = total + from_a[j].astype(jnp.float32)
            if j > 0:
                part[mine] = total.astype(jnp.bfloat16)
                (b_copy(j - 8) if j >= 8 else a_copy(j - 4) if j >= 4 else z_copy(j)).start()
            else:
                for k in (1, 2, 3):
                    z_copy(k).wait_recv()
                    total = total + from_z[k].astype(jnp.float32)
                result = (residual[...] + total).astype(jnp.bfloat16)
                out[step] = result
                carried[...] = result.astype(jnp.float32)[:BLOCK]
        for j in range(16):
            core_copy(j).wait_send()
        for j in range(8):
            b_copy(j).wait_send()
        for j in range(4):
            a_copy(j).wait_send()
        for k in (1, 2, 3):
            z_copy(k).wait_send()
        return 0

    lax.fori_loop(0, 2, one_step, 0)


def on_device_close(
    cache_keys, cache_values, lengths, drift_rows, block_in, drift_in, queries, new_keys,
    new_values, norm_gain, expert_ids, gate_weights, w_gate, w_up, w_down,
):
    attended = attend_both(
        cache_keys[0],
        cache_values[0],
        lengths[0],
        drift_rows[:, 0],
        queries[:, 0],
        new_keys[:, 0],
        new_values[:, 0],
    )
    row_count, width = queries.shape[2], queries.shape[3]
    first = jnp.stack([block_in[0], jnp.zeros_like(block_in[0])])
    base = attended + jnp.concatenate([first, drift_in[:, 0]], axis=1).astype(jnp.float32)
    member = expert_ids[:, 0, :, :, None] == jnp.arange(128)
    tables = jnp.sum(jnp.where(member, gate_weights[:, 0, :, :, None], 0), axis=2)
    tables = tables.astype(jnp.bfloat16)
    vmem = pl.BlockSpec(memory_space=pltpu.VMEM)
    hbm = pl.BlockSpec(memory_space=pl.ANY)
    block = (row_count, width)
    bf16 = jnp.bfloat16
    out = pl.pallas_call(
        expert_kernel,
        out_shape=jax.ShapeDtypeStruct((2, row_count, width), bf16),
        in_specs=[vmem, vmem, vmem, hbm, hbm, hbm],
        out_specs=vmem,
        scratch_shapes=[
            pltpu.VMEM((SLOTS, row_count, width + 128), bf16),
            pltpu.VMEM((SLOTS, *block), bf16),
            pltpu.VMEM((16 * row_count, w_down.shape[1]), bf16),
            pltpu.VMEM((16, *block), bf16),
            pltpu.VMEM((8, *block), bf16),
            pltpu.VMEM((4, *block), bf16),
            pltpu.VMEM((4, *block), bf16),
            pltpu.VMEM(block, jnp.float32),
            pltpu.VMEM((BLOCK, width), jnp.float32),
            pltpu.VMEM(w_gate.shape[1:], bf16),
            pltpu.VMEM(w_up.shape[1:], bf16),
            pltpu.VMEM(w_down.shape[1:], bf16),
            pltpu.SemaphoreType.DMA((3,)),
            pltpu.SemaphoreType.DMA((SLOTS,)),
            pltpu.SemaphoreType.DMA((SLOTS,)),
            pltpu.SemaphoreType.DMA((SLOTS,)),
            pltpu.SemaphoreType.DMA((SLOTS,)),
        ],
        compiler_params=pltpu.CompilerParams(
            collective_id=0, has_side_effects=True, vmem_limit_bytes=60 * 2**20
        ),
        name="experts",
    )(base, tables, norm_gain[None], w_gate[0], w_up[0], w_down[0])
    return out[:, None]


def solution(mesh):
    close = mesh.shape["rep"] == 2 and mesh.shape["exp"] == 16
    placed = (
        P(("rep", "exp"), None, None),
        P(("rep", "exp"), None, None),
        P(("rep", "exp")),
        P(None, ("rep", "exp"), None),
        P(("rep", "exp"), None, None),
        P(None, ("rep", "exp"), None, None),
        P(None, ("rep", "exp"), None, None),
        P(None, ("rep", "exp"), None, None),
        P(None, ("rep", "exp"), None, None),
        P(),
        P(None, ("rep", "exp"), None, None),
        P(None, ("rep", "exp"), None, None),
        P("exp", None, "rep"),
        P("exp", None, "rep"),
        P("exp", "rep", None),
    )
    return jax.shard_map(
        on_device_close if close else on_device,
        mesh=mesh,
        in_specs=placed,
        out_specs=P(None, ("rep", "exp"), None, None),
        check_vma=False,
    )
```

```python
import jax
import jax.numpy as jnp
from jax import lax
from jax.experimental import pallas as pl
from jax.experimental.pallas import tpu as pltpu
from jax.sharding import PartitionSpec as P

H = 32
KVH = 4
HD = 128
TOP = 8
BLOCK = 8


def attend(query_rows, key_rows, value_rows, block_keys, block_values, length):
    row_count = query_rows.shape[0]
    group_size = H // KVH
    query_head_rows = query_rows.reshape(row_count, KVH, group_size, HD)
    cache_k = key_rows.reshape(-1, KVH, HD)
    cached_value_rows = value_rows.reshape(-1, KVH, HD)
    prompt_key_rows = block_keys.reshape(-1, KVH, HD)
    prompt_value_rows = block_values.reshape(-1, KVH, HD)
    logit_scale_factor = HD ** (-0.5)
    cache_scores = (
        jnp.einsum("rkgd,ckd->kgrc", query_head_rows, cache_k, preferred_element_type=jnp.float32)
        * logit_scale_factor
    )
    prompt_score_rows = (
        jnp.einsum(
            "afhu,nfu->fhan", query_head_rows, prompt_key_rows, preferred_element_type=jnp.float32
        )
        * logit_scale_factor
    )
    cache_mask = jnp.arange(cache_k.shape[0]) < length
    own_mask = (jnp.arange(row_count) < BLOCK)[:, None]
    cache_scores = jnp.where(cache_mask, cache_scores, -1e30)
    prompt_score_rows = jnp.where(own_mask, prompt_score_rows, -1e30)
    peak = jnp.maximum(jnp.max(cache_scores, axis=-1), jnp.max(prompt_score_rows, axis=-1))
    cache_exp = jnp.exp(cache_scores - peak[..., None])
    own_exp = jnp.exp(prompt_score_rows - peak[..., None])
    denom = jnp.sum(cache_exp, axis=-1) + jnp.sum(own_exp, axis=-1)
    cached_weight_share = (cache_exp / denom[..., None]).astype(jnp.bfloat16)
    prompt_weight_share = (own_exp / denom[..., None]).astype(jnp.bfloat16)
    blended_output = jnp.einsum(
        "qimt,tqj->mqij", cached_weight_share, cached_value_rows, preferred_element_type=jnp.float32
    )
    blended_output = blended_output + jnp.einsum(
        "iywf,fie->wiye", prompt_weight_share, prompt_value_rows, preferred_element_type=jnp.float32
    )
    return blended_output.reshape(row_count, H * HD)


def route_table(routed, gate_share, experts, capacity):
    member = routed[:, :, None] == jnp.arange(experts)[None, None, :]
    weight = jnp.sum(jnp.where(member, gate_share[:, :, None].astype(jnp.float32), 0.0), axis=1)
    chosen = jnp.any(member, axis=1).astype(jnp.int32)
    slot_rank = jnp.cumsum(chosen, axis=0) - chosen
    taken = (slot_rank[:, :, None] == jnp.arange(capacity)[None, None, :]) & (
        chosen[:, :, None] == 1
    )
    return jnp.where(taken, weight[:, :, None], 0.0).astype(jnp.bfloat16)


def expert_terms(routed_rows, gate_part, up_part, down_part):
    flat_rows = routed_rows.reshape(-1, routed_rows.shape[-1])
    gate_act = jnp.dot(flat_rows, gate_part, preferred_element_type=jnp.float32)
    up_act = jnp.dot(flat_rows, up_part, preferred_element_type=jnp.float32)
    hidden = (jax.nn.silu(gate_act) * up_act).astype(jnp.bfloat16)
    produced = jnp.dot(hidden, down_part, preferred_element_type=jnp.float32).astype(jnp.bfloat16)
    return produced.reshape(routed_rows.shape)


def on_device(
    cache_keys,
    cache_values,
    lengths,
    drift_rows,
    block_in,
    drift_in,
    queries,
    new_keys,
    new_values,
    norm_gain,
    expert_ids,
    gate_weights,
    w_gate,
    w_up,
    w_down,
):
    rep_count = lax.axis_size("rep")
    experts = lax.axis_size("exp") * w_gate.shape[0]
    row_count = queries.shape[2]
    capacity = min(row_count, (3 * row_count * TOP + 2 * experts - 1) // (2 * experts))
    key_rows = cache_keys[0]
    value_rows = cache_values[0]
    carried = block_in[0]
    results = []
    for denoise in range(2):
        key_rows = key_rows.at[drift_rows[denoise, 0]].set(new_keys[denoise, 0, BLOCK:])
        value_rows = value_rows.at[drift_rows[denoise, 0]].set(new_values[denoise, 0, BLOCK:])
        attended = attend(
            queries[denoise, 0],
            key_rows,
            value_rows,
            new_keys[denoise, 0, :BLOCK],
            new_values[denoise, 0, :BLOCK],
            lengths[0],
        )
        inputs = jnp.concatenate([carried, drift_in[denoise, 0]], axis=0).astype(jnp.float32)
        residual = inputs + attended
        inverse = lax.rsqrt(jnp.mean(residual * residual, axis=-1, keepdims=True) + 1e-06)
        normed = (residual * inverse * norm_gain).astype(jnp.bfloat16)
        slot_table = route_table(
            expert_ids[denoise, 0], gate_weights[denoise, 0], experts, capacity
        )
        flat_table = slot_table.reshape(row_count, experts * capacity)
        all_rows, all_tables = (
            lax.all_gather(normed, "rep", axis=0, tiled=True),
            lax.all_gather(flat_table, "rep", axis=0, tiled=True),
        )
        all_rows = all_rows.reshape(rep_count, row_count, -1)
        all_tables = all_tables.reshape(rep_count, row_count, experts, capacity)
        chosen_slots = (all_tables != 0).astype(jnp.bfloat16)
        dispatched = jnp.einsum(
            "orec,ord->eocd", chosen_slots, all_rows, preferred_element_type=jnp.float32
        ).astype(jnp.bfloat16)
        produced = expert_terms(
            lax.all_to_all(dispatched, "exp", split_axis=0, concat_axis=0, tiled=True),
            w_gate[0],
            w_up[0],
            w_down[0],
        )
        expert_out = lax.all_to_all(produced, "exp", split_axis=0, concat_axis=0, tiled=True)
        combined = jnp.einsum(
            "orec,eocd->ord", all_tables, expert_out, preferred_element_type=jnp.float32
        )
        moe = lax.psum_scatter(
            combined.reshape(rep_count * row_count, -1).astype(jnp.bfloat16),
            "rep",
            scatter_dimension=0,
            tiled=True,
        ).astype(jnp.float32)
        result = (residual + moe).astype(jnp.bfloat16)
        results.append(result)
        carried = result[:BLOCK]
    return jnp.stack(results)[:, None]


GROUP = H // KVH
EXTRA = 128


def attention_kernel(q_ref, k_ref, v_ref, xk_ref, xv_ref, mask_ref, xmask_ref, out_ref):
    scale = HD ** (-0.5)
    keys, values = k_ref[...], v_ref[...]
    row_count = q_ref.shape[1]
    for step in range(2):
        q = jnp.concatenate(
            [q_ref[step, :, g * HD : (g + 1) * HD] for g in range(GROUP)], axis=0
        )
        nt = (((1,), (1,)), ((), ()))
        scores = lax.dot_general(q, keys, nt, preferred_element_type=jnp.float32)
        scores = scores * scale + mask_ref[step]
        extra = lax.dot_general(q, xk_ref[step], nt, preferred_element_type=jnp.float32)
        extra = extra * scale + xmask_ref[step]
        peak = jnp.maximum(
            jnp.max(scores, axis=1, keepdims=True), jnp.max(extra, axis=1, keepdims=True)
        )
        scores = jnp.exp(scores - peak)
        extra = jnp.exp(extra - peak)
        denom = jnp.sum(scores, axis=1, keepdims=True) + jnp.sum(extra, axis=1, keepdims=True)
        mixed = jnp.dot(scores.astype(jnp.bfloat16), values, preferred_element_type=jnp.float32)
        mixed += jnp.dot(
            extra.astype(jnp.bfloat16), xv_ref[step], preferred_element_type=jnp.float32
        )
        mixed = mixed / denom
        for g in range(GROUP):
            out_ref[step, :, g * HD : (g + 1) * HD] = mixed[g * row_count : (g + 1) * row_count]


def attend_both(keys, values, length, drift, queries, new_keys, new_values):
    row_count, slots = queries.shape[1], keys.shape[0]
    places = jnp.arange(slots)
    hit = jnp.any(places[None, None, :] == drift[:, :, None], axis=1)
    valid = places < length
    open_ = jnp.stack([valid & ~hit[0], valid & ~hit[0] & ~hit[1]])
    mask = jnp.where(open_, 0.0, -1e30).astype(jnp.float32)[:, None, :]
    kept = ~jnp.any(drift[0][:, None] == drift[1][None, :], axis=1)
    own = (jnp.arange(row_count) < BLOCK)[None, :, None]
    own = jnp.broadcast_to(own, (2, row_count, BLOCK))
    fresh = jnp.ones((2, row_count, row_count - BLOCK), bool)
    older = jnp.stack([jnp.zeros_like(kept), kept])[:, None, :]
    older = jnp.broadcast_to(older, (2, row_count, kept.shape[0]))
    rest = jnp.zeros((2, row_count, EXTRA - row_count - kept.shape[0]), bool)
    xmask = jnp.where(jnp.concatenate([own, fresh, older, rest], axis=2), 0.0, -1e30)
    xmask = jnp.tile(xmask.astype(jnp.float32), (1, GROUP, 1))

    def extras(new):
        again = jnp.broadcast_to(new[:1, BLOCK:], (2, row_count - BLOCK, new.shape[2]))
        joined = jnp.concatenate([new, again], axis=1)
        return jnp.pad(joined, ((0, 0), (0, EXTRA - joined.shape[1]), (0, 0)))

    wide = GROUP * HD
    return pl.pallas_call(
        attention_kernel,
        grid=(KVH,),
        in_specs=[
            pl.BlockSpec((2, row_count, wide), lambda j: (0, 0, j)),
            pl.BlockSpec((slots, HD), lambda j: (0, j)),
            pl.BlockSpec((slots, HD), lambda j: (0, j)),
            pl.BlockSpec((2, EXTRA, HD), lambda j: (0, 0, j)),
            pl.BlockSpec((2, EXTRA, HD), lambda j: (0, 0, j)),
            pl.BlockSpec((2, 1, slots), lambda j: (0, 0, 0)),
            pl.BlockSpec((2, GROUP * row_count, EXTRA), lambda j: (0, 0, 0)),
        ],
        out_specs=pl.BlockSpec((2, row_count, wide), lambda j: (0, 0, j)),
        out_shape=jax.ShapeDtypeStruct((2, row_count, H * HD), jnp.float32),
        compiler_params=pltpu.CompilerParams(vmem_limit_bytes=60 * 2**20),
        name="attention",
    )(queries, keys, values, extras(new_keys), extras(new_values), mask, xmask)


SLOTS = 32


def expert_kernel(
    base, tables, gain, wg_in, wu_in, wd_in, out,
    rows, part, hidden, from_core, from_b, from_a, from_z, residual, carried, wg, wu, wd,
    w_sem, ag_send, ag_recv, rs_send, rs_recv,
):
    y, e = lax.axis_index("rep"), lax.axis_index("exp")
    c, x, z = lax.rem(e, 2), lax.rem(lax.div(e, 2), 2), lax.div(e, 4)
    z_low, z_high = lax.rem(z, 2), lax.div(z, 2)

    def device(y_, z_, x_, c_):
        return (y_, (z_ * 2 + x_) * 2 + c_)

    core = device(y, z, x, 1 - c)
    a_side = device(y + c * (1 - 2 * y), z, x + (1 - c) * (1 - 2 * x), c)
    b_side = device(y + (1 - c) * (1 - 2 * y), z, x + c * (1 - 2 * x), c)
    z_side = [None] + [
        device(
            y,
            ((1 - z_high) if k & 2 else z_high) * 2 + ((1 - z_low) if k & 1 else z_low),
            x,
            c,
        )
        for k in (1, 2, 3)
    ]

    loads = [
        pltpu.make_async_copy(src, dst, w_sem.at[i])
        for i, (src, dst) in enumerate(((wg_in, wg), (wu_in, wu), (wd_in, wd)))
    ]
    for load in loads:
        load.start()

    barrier = pltpu.get_barrier_semaphore()
    for peer in (core, a_side, b_side, *z_side[1:]):
        pl.semaphore_signal(barrier, inc=1, device_id=peer, device_id_type=pl.DeviceIdType.MESH)
    pl.semaphore_wait(barrier, 6)

    def remote(src, dst, send, recv, peer):
        return pltpu.make_async_remote_copy(
            src_ref=src,
            dst_ref=dst,
            send_sem=send,
            recv_sem=recv,
            device_id=peer,
            device_id_type=pl.DeviceIdType.MESH,
        )

    def gather_copy(d):
        if d & 8:
            src, peer = d - 8, core
        elif d & 4:
            src, peer = d - 4, b_side
        elif d & 2:
            src, peer = d - 2, a_side
        else:
            src, peer = 0, z_side[d // 8 + d % 2]
        return remote(rows.at[src], rows.at[d], ag_send.at[d], ag_recv.at[d], peer)

    def core_copy(j):
        src = part.at[j // 8 * 16 + 8 + j % 8]
        return remote(src, from_core.at[j], rs_send.at[j], rs_recv.at[j], core)

    def b_copy(j):
        src = part.at[j // 4 * 16 + 4 + j % 4]
        return remote(src, from_b.at[j], rs_send.at[16 + j], rs_recv.at[16 + j], b_side)

    def a_copy(j):
        src = part.at[j // 2 * 16 + 2 + j % 2]
        return remote(src, from_a.at[j], rs_send.at[24 + j], rs_recv.at[24 + j], a_side)

    def z_copy(k):
        src = part.at[k // 2 * 16 + k % 2]
        return remote(src, from_z.at[k], rs_send.at[28 + k], rs_recv.at[28 + k], z_side[k])

    width = wd.shape[1]
    tile = 256
    row_count = rows.shape[1]
    half = 16 * row_count

    def up_tile(first, n):
        span = pl.ds(first, 16)
        share = rows[span, :, width:].reshape(half, rows.shape[2] - width).astype(jnp.float32)
        lane = lax.broadcasted_iota(jnp.int32, share.shape, 1)
        share = jnp.sum(jnp.where(lane == e, share, 0.0), axis=1, keepdims=True)
        columns = pl.ds(n * tile, tile)
        x_rows = rows[span, :, :width].reshape(half, width)
        gate = jnp.dot(x_rows, wg[:, columns], preferred_element_type=jnp.float32)
        up = jnp.dot(x_rows, wu[:, columns], preferred_element_type=jnp.float32)
        act = gate / (1.0 + jnp.exp(-gate)) * up * share
        hidden[pl.ds(first * row_count, half), columns] = act.astype(jnp.bfloat16)

    def down(first):
        span = pl.ds(first, 8)

        def down_tile(n, _):
            columns = pl.ds(pl.multiple_of(n * 512, 512), 512)
            made = jnp.dot(
                hidden[pl.ds(first * row_count, half // 2)],
                wd[:, columns],
                preferred_element_type=jnp.float32,
            )
            part[span, :, columns] = made.astype(jnp.bfloat16).reshape(8, row_count, 512)
            return 0

        lax.fori_loop(0, width // 512, down_tile, 0)

    carried[...] = jnp.zeros_like(carried)

    def one_step(step, _):
        residual[...] = base[step]
        residual[:BLOCK] = residual[:BLOCK] + carried[...]
        held = residual[...]
        inverse = lax.rsqrt(jnp.mean(held * held, axis=1, keepdims=True) + 1e-06)
        rows[0, :, :width] = (held * inverse * gain[...]).astype(jnp.bfloat16)
        rows[0, :, width:] = tables[step]

        def forward(d):
            if d & 6 == 0:
                gather_copy(2 + d).start()
            if d & 4 == 0:
                gather_copy(4 + d).start()
            gather_copy(8 + d).start()

        def pass_on(*slots):
            for d in slots:
                gather_copy(d).wait_recv()
                forward(d)

        for d in (1, 16, 17):
            gather_copy(d).start()
        forward(0)
        pass_on(2, 1, 4, 3, 5, 16, 6, 18, 7)

        @pl.when(step == 0)
        def _():
            for load in loads:
                load.wait()

        for d in range(8, 16):
            gather_copy(d).wait_recv()
        up_tile(0, 0)
        pass_on(17, 20)
        up_tile(0, 1)
        pass_on(19, 22, 21, 23)
        for d in range(24, SLOTS):
            gather_copy(d).wait_recv()
        up_tile(16, 0)
        up_tile(16, 1)
        for d in range(1, SLOTS):
            gather_copy(d).wait_send()

        def summed(z_half, r):
            j, mine = z_half * 8 + r, z_half * 16 + r
            core_copy(j).wait_recv()
            total = part[mine].astype(jnp.float32) + from_core[j].astype(jnp.float32)
            if r < 4:
                b_copy(z_half * 4 + r).wait_recv()
                total = total + from_b[z_half * 4 + r].astype(jnp.float32)
            if r < 2:
                a_copy(z_half * 2 + r).wait_recv()
                total = total + from_a[z_half * 2 + r].astype(jnp.float32)
            return total

        def hand_on(z_half, *places):
            for r in places:
                part[z_half * 16 + r] = summed(z_half, r).astype(jnp.bfloat16)
                if r >= 4:
                    b_copy(z_half * 4 + r - 4).start()
                elif r >= 2:
                    a_copy(z_half * 2 + r - 2).start()
                else:
                    z_copy(z_half * 2 + r).start()

        order = (7, 5, 6, 4, 3, 1, 2, 0)
        down(24)
        for r in order:
            core_copy(8 + r).start()
        down(16)
        hand_on(1, 7, 5, 6, 4)
        down(8)
        for r in order:
            core_copy(r).start()
        hand_on(1, 3)
        down(0)
        hand_on(0, 7, 5)
        hand_on(1, 2, 1)
        hand_on(0, 6, 4)
        hand_on(1, 0)
        hand_on(0, 3, 2, 1)
        total = summed(0, 0)
        for k in (1, 2, 3):
            z_copy(k).wait_recv()
            total = total + from_z[k].astype(jnp.float32)
        result = (residual[...] + total).astype(jnp.bfloat16)
        out[step] = result
        carried[...] = result.astype(jnp.float32)[:BLOCK]
        for j in range(16):
            core_copy(j).wait_send()
        for j in range(8):
            b_copy(j).wait_send()
        for j in range(4):
            a_copy(j).wait_send()
        for k in (1, 2, 3):
            z_copy(k).wait_send()
        return 0

    lax.fori_loop(0, 2, one_step, 0)


def on_device_close(
    cache_keys, cache_values, lengths, drift_rows, block_in, drift_in, queries, new_keys,
    new_values, norm_gain, expert_ids, gate_weights, w_gate, w_up, w_down,
):
    attended = attend_both(
        cache_keys[0],
        cache_values[0],
        lengths[0],
        drift_rows[:, 0],
        queries[:, 0],
        new_keys[:, 0],
        new_values[:, 0],
    )
    row_count, width = queries.shape[2], queries.shape[3]
    first = jnp.stack([block_in[0], jnp.zeros_like(block_in[0])])
    base = attended + jnp.concatenate([first, drift_in[:, 0]], axis=1).astype(jnp.float32)
    member = expert_ids[:, 0, :, :, None] == jnp.arange(128)
    tables = jnp.sum(jnp.where(member, gate_weights[:, 0, :, :, None], 0), axis=2)
    tables = tables.astype(jnp.bfloat16)
    vmem = pl.BlockSpec(memory_space=pltpu.VMEM)
    hbm = pl.BlockSpec(memory_space=pl.ANY)
    block = (row_count, width)
    bf16 = jnp.bfloat16
    out = pl.pallas_call(
        expert_kernel,
        out_shape=jax.ShapeDtypeStruct((2, row_count, width), bf16),
        in_specs=[vmem, vmem, vmem, hbm, hbm, hbm],
        out_specs=vmem,
        scratch_shapes=[
            pltpu.VMEM((SLOTS, row_count, width + 128), bf16),
            pltpu.VMEM((SLOTS, *block), bf16),
            pltpu.VMEM((SLOTS * row_count, w_down.shape[1]), bf16),
            pltpu.VMEM((16, *block), bf16),
            pltpu.VMEM((8, *block), bf16),
            pltpu.VMEM((4, *block), bf16),
            pltpu.VMEM((4, *block), bf16),
            pltpu.VMEM(block, jnp.float32),
            pltpu.VMEM((BLOCK, width), jnp.float32),
            pltpu.VMEM(w_gate.shape[1:], bf16),
            pltpu.VMEM(w_up.shape[1:], bf16),
            pltpu.VMEM(w_down.shape[1:], bf16),
            pltpu.SemaphoreType.DMA((3,)),
            pltpu.SemaphoreType.DMA((SLOTS,)),
            pltpu.SemaphoreType.DMA((SLOTS,)),
            pltpu.SemaphoreType.DMA((SLOTS,)),
            pltpu.SemaphoreType.DMA((SLOTS,)),
        ],
        compiler_params=pltpu.CompilerParams(
            collective_id=0, has_side_effects=True, vmem_limit_bytes=60 * 2**20
        ),
        name="experts",
    )(base, tables, norm_gain[None], w_gate[0], w_up[0], w_down[0])
    return out[:, None]


def solution(mesh):
    close = mesh.shape["rep"] == 2 and mesh.shape["exp"] == 16
    placed = (
        P(("rep", "exp"), None, None),
        P(("rep", "exp"), None, None),
        P(("rep", "exp")),
        P(None, ("rep", "exp"), None),
        P(("rep", "exp"), None, None),
        P(None, ("rep", "exp"), None, None),
        P(None, ("rep", "exp"), None, None),
        P(None, ("rep", "exp"), None, None),
        P(None, ("rep", "exp"), None, None),
        P(),
        P(None, ("rep", "exp"), None, None),
        P(None, ("rep", "exp"), None, None),
        P("exp", None, "rep"),
        P("exp", None, "rep"),
        P("exp", "rep", None),
    )
    return jax.shard_map(
        on_device_close if close else on_device,
        mesh=mesh,
        in_specs=placed,
        out_specs=P(None, ("rep", "exp"), None, None),
        check_vma=False,
    )
```

```python
import jax
import jax.numpy as jnp
from jax import lax
from jax.experimental import pallas as pl
from jax.experimental.pallas import tpu as pltpu
from jax.sharding import PartitionSpec as P

H = 32
KVH = 4
HD = 128
TOP = 8
BLOCK = 8


def attend(query_rows, key_rows, value_rows, block_keys, block_values, length):
    row_count = query_rows.shape[0]
    group_size = H // KVH
    query_head_rows = query_rows.reshape(row_count, KVH, group_size, HD)
    cache_k = key_rows.reshape(-1, KVH, HD)
    cached_value_rows = value_rows.reshape(-1, KVH, HD)
    prompt_key_rows = block_keys.reshape(-1, KVH, HD)
    prompt_value_rows = block_values.reshape(-1, KVH, HD)
    logit_scale_factor = HD ** (-0.5)
    cache_scores = (
        jnp.einsum("rkgd,ckd->kgrc", query_head_rows, cache_k, preferred_element_type=jnp.float32)
        * logit_scale_factor
    )
    prompt_score_rows = (
        jnp.einsum(
            "afhu,nfu->fhan", query_head_rows, prompt_key_rows, preferred_element_type=jnp.float32
        )
        * logit_scale_factor
    )
    cache_mask = jnp.arange(cache_k.shape[0]) < length
    own_mask = (jnp.arange(row_count) < BLOCK)[:, None]
    cache_scores = jnp.where(cache_mask, cache_scores, -1e30)
    prompt_score_rows = jnp.where(own_mask, prompt_score_rows, -1e30)
    peak = jnp.maximum(jnp.max(cache_scores, axis=-1), jnp.max(prompt_score_rows, axis=-1))
    cache_exp = jnp.exp(cache_scores - peak[..., None])
    own_exp = jnp.exp(prompt_score_rows - peak[..., None])
    denom = jnp.sum(cache_exp, axis=-1) + jnp.sum(own_exp, axis=-1)
    cached_weight_share = (cache_exp / denom[..., None]).astype(jnp.bfloat16)
    prompt_weight_share = (own_exp / denom[..., None]).astype(jnp.bfloat16)
    blended_output = jnp.einsum(
        "qimt,tqj->mqij", cached_weight_share, cached_value_rows, preferred_element_type=jnp.float32
    )
    blended_output = blended_output + jnp.einsum(
        "iywf,fie->wiye", prompt_weight_share, prompt_value_rows, preferred_element_type=jnp.float32
    )
    return blended_output.reshape(row_count, H * HD)


def route_table(routed, gate_share, experts, capacity):
    member = routed[:, :, None] == jnp.arange(experts)[None, None, :]
    weight = jnp.sum(jnp.where(member, gate_share[:, :, None].astype(jnp.float32), 0.0), axis=1)
    chosen = jnp.any(member, axis=1).astype(jnp.int32)
    slot_rank = jnp.cumsum(chosen, axis=0) - chosen
    taken = (slot_rank[:, :, None] == jnp.arange(capacity)[None, None, :]) & (
        chosen[:, :, None] == 1
    )
    return jnp.where(taken, weight[:, :, None], 0.0).astype(jnp.bfloat16)


def expert_terms(routed_rows, gate_part, up_part, down_part):
    flat_rows = routed_rows.reshape(-1, routed_rows.shape[-1])
    gate_act = jnp.dot(flat_rows, gate_part, preferred_element_type=jnp.float32)
    up_act = jnp.dot(flat_rows, up_part, preferred_element_type=jnp.float32)
    hidden = (jax.nn.silu(gate_act) * up_act).astype(jnp.bfloat16)
    produced = jnp.dot(hidden, down_part, preferred_element_type=jnp.float32).astype(jnp.bfloat16)
    return produced.reshape(routed_rows.shape)


def on_device(
    cache_keys,
    cache_values,
    lengths,
    drift_rows,
    block_in,
    drift_in,
    queries,
    new_keys,
    new_values,
    norm_gain,
    expert_ids,
    gate_weights,
    w_gate,
    w_up,
    w_down,
):
    rep_count = lax.axis_size("rep")
    experts = lax.axis_size("exp") * w_gate.shape[0]
    row_count = queries.shape[2]
    capacity = min(row_count, (3 * row_count * TOP + 2 * experts - 1) // (2 * experts))
    key_rows = cache_keys[0]
    value_rows = cache_values[0]
    carried = block_in[0]
    results = []
    for denoise in range(2):
        key_rows = key_rows.at[drift_rows[denoise, 0]].set(new_keys[denoise, 0, BLOCK:])
        value_rows = value_rows.at[drift_rows[denoise, 0]].set(new_values[denoise, 0, BLOCK:])
        attended = attend(
            queries[denoise, 0],
            key_rows,
            value_rows,
            new_keys[denoise, 0, :BLOCK],
            new_values[denoise, 0, :BLOCK],
            lengths[0],
        )
        inputs = jnp.concatenate([carried, drift_in[denoise, 0]], axis=0).astype(jnp.float32)
        residual = inputs + attended
        inverse = lax.rsqrt(jnp.mean(residual * residual, axis=-1, keepdims=True) + 1e-06)
        normed = (residual * inverse * norm_gain).astype(jnp.bfloat16)
        slot_table = route_table(
            expert_ids[denoise, 0], gate_weights[denoise, 0], experts, capacity
        )
        flat_table = slot_table.reshape(row_count, experts * capacity)
        all_rows, all_tables = (
            lax.all_gather(normed, "rep", axis=0, tiled=True),
            lax.all_gather(flat_table, "rep", axis=0, tiled=True),
        )
        all_rows = all_rows.reshape(rep_count, row_count, -1)
        all_tables = all_tables.reshape(rep_count, row_count, experts, capacity)
        chosen_slots = (all_tables != 0).astype(jnp.bfloat16)
        dispatched = jnp.einsum(
            "orec,ord->eocd", chosen_slots, all_rows, preferred_element_type=jnp.float32
        ).astype(jnp.bfloat16)
        produced = expert_terms(
            lax.all_to_all(dispatched, "exp", split_axis=0, concat_axis=0, tiled=True),
            w_gate[0],
            w_up[0],
            w_down[0],
        )
        expert_out = lax.all_to_all(produced, "exp", split_axis=0, concat_axis=0, tiled=True)
        combined = jnp.einsum(
            "orec,eocd->ord", all_tables, expert_out, preferred_element_type=jnp.float32
        )
        moe = lax.psum_scatter(
            combined.reshape(rep_count * row_count, -1).astype(jnp.bfloat16),
            "rep",
            scatter_dimension=0,
            tiled=True,
        ).astype(jnp.float32)
        result = (residual + moe).astype(jnp.bfloat16)
        results.append(result)
        carried = result[:BLOCK]
    return jnp.stack(results)[:, None]


GROUP = H // KVH


def attention_kernel(
    q_ref, k_ref, v_ref, nk_ref, nv_ref, mask_ref, xmask_ref, first_ref, drift_ref, out_ref
):
    scale = HD ** (-0.5)
    keys, values = k_ref[...], v_ref[...]
    row_count = q_ref.shape[1]
    for step in range(2):
        q = jnp.concatenate(
            [q_ref[step, :, g * HD : (g + 1) * HD] for g in range(GROUP)], axis=0
        )
        nt = (((1,), (1,)), ((), ()))
        scores = lax.dot_general(q, keys, nt, preferred_element_type=jnp.float32)
        scores = scores * scale + mask_ref[step]
        extra_keys = jnp.concatenate([nk_ref[step], nk_ref[0]], axis=0)
        extra_values = jnp.concatenate([nv_ref[step], nv_ref[0]], axis=0)
        extra = lax.dot_general(q, extra_keys, nt, preferred_element_type=jnp.float32)
        extra = extra * scale + xmask_ref[step]
        peak = jnp.maximum(
            jnp.max(scores, axis=1, keepdims=True), jnp.max(extra, axis=1, keepdims=True)
        )
        scores = jnp.exp(scores - peak)
        extra = jnp.exp(extra - peak)
        denom = jnp.sum(scores, axis=1, keepdims=True) + jnp.sum(extra, axis=1, keepdims=True)
        mixed = jnp.dot(scores.astype(jnp.bfloat16), values, preferred_element_type=jnp.float32)
        mixed += jnp.dot(
            extra.astype(jnp.bfloat16), extra_values, preferred_element_type=jnp.float32
        )
        mixed = mixed / denom
        for g in range(GROUP):
            columns = slice(g * HD, (g + 1) * HD)
            block = mixed[g * row_count : g * row_count + BLOCK]
            if step == 0:
                block = block + first_ref[:, columns].astype(jnp.float32)
            drifted = mixed[g * row_count + BLOCK : (g + 1) * row_count]
            out_ref[step, :BLOCK, columns] = block
            out_ref[step, BLOCK:, columns] = drifted + drift_ref[step, :, columns].astype(jnp.float32)


def attend_both(keys, values, length, drift, queries, new_keys, new_values, first, drift_in):
    row_count, slots = queries.shape[1], keys.shape[0]
    places = jnp.arange(slots)
    hit = jnp.any(places[None, None, :] == drift[:, :, None], axis=1)
    valid = places < length
    open_ = jnp.stack([valid & ~hit[0], valid & ~hit[0] & ~hit[1]])
    mask = jnp.where(open_, 0.0, -1e30).astype(jnp.float32)[:, None, :]
    kept = ~jnp.any(drift[0][:, None] == drift[1][None, :], axis=1)
    own = (jnp.arange(row_count) < BLOCK)[None, :, None]
    own = jnp.broadcast_to(own, (2, row_count, BLOCK))
    fresh = jnp.ones((2, row_count, row_count - BLOCK), bool)
    older = jnp.stack([jnp.zeros_like(kept), kept])[:, None, :]
    older = jnp.broadcast_to(older, (2, row_count, kept.shape[0]))
    none = jnp.zeros((2, row_count, BLOCK), bool)
    xmask = jnp.where(jnp.concatenate([own, fresh, none, older], axis=2), 0.0, -1e30)
    xmask = jnp.tile(xmask.astype(jnp.float32), (1, GROUP, 1))

    wide = GROUP * HD
    return pl.pallas_call(
        attention_kernel,
        grid=(KVH,),
        in_specs=[
            pl.BlockSpec((2, row_count, wide), lambda j: (0, 0, j)),
            pl.BlockSpec((slots, HD), lambda j: (0, j)),
            pl.BlockSpec((slots, HD), lambda j: (0, j)),
            pl.BlockSpec((2, row_count, HD), lambda j: (0, 0, j)),
            pl.BlockSpec((2, row_count, HD), lambda j: (0, 0, j)),
            pl.BlockSpec((2, 1, slots), lambda j: (0, 0, 0)),
            pl.BlockSpec((2, GROUP * row_count, 2 * row_count), lambda j: (0, 0, 0)),
            pl.BlockSpec((BLOCK, wide), lambda j: (0, j)),
            pl.BlockSpec((2, row_count - BLOCK, wide), lambda j: (0, 0, j)),
        ],
        out_specs=pl.BlockSpec((2, row_count, wide), lambda j: (0, 0, j)),
        out_shape=jax.ShapeDtypeStruct((2, row_count, H * HD), jnp.float32),
        compiler_params=pltpu.CompilerParams(vmem_limit_bytes=60 * 2**20),
        name="attention",
    )(queries, keys, values, new_keys, new_values, mask, xmask, first, drift_in)


SLOTS = 32


def expert_kernel(
    base, tables, gain, wg_in, wu_in, wd_in, out,
    rows, part, hidden, from_core, from_b, from_a, from_z, residual, carried, wg, wu, wd,
    w_sem, ag_send, ag_recv, rs_send, rs_recv,
):
    y, e = lax.axis_index("rep"), lax.axis_index("exp")
    c, x, z = lax.rem(e, 2), lax.rem(lax.div(e, 2), 2), lax.div(e, 4)
    z_low, z_high = lax.rem(z, 2), lax.div(z, 2)

    def device(y_, z_, x_, c_):
        return (y_, (z_ * 2 + x_) * 2 + c_)

    core = device(y, z, x, 1 - c)
    a_side = device(y + c * (1 - 2 * y), z, x + (1 - c) * (1 - 2 * x), c)
    b_side = device(y + (1 - c) * (1 - 2 * y), z, x + c * (1 - 2 * x), c)
    z_side = [None] + [
        device(
            y,
            ((1 - z_high) if k & 2 else z_high) * 2 + ((1 - z_low) if k & 1 else z_low),
            x,
            c,
        )
        for k in (1, 2)
    ]

    loads = [
        pltpu.make_async_copy(src, dst, w_sem.at[i])
        for i, (src, dst) in enumerate(((wg_in, wg), (wu_in, wu), (wd_in, wd)))
    ]
    for load in loads:
        load.start()

    barrier = pltpu.get_barrier_semaphore()
    for peer in (core, a_side, b_side, *z_side[1:]):
        pl.semaphore_signal(barrier, inc=1, device_id=peer, device_id_type=pl.DeviceIdType.MESH)
    pl.semaphore_wait(barrier, 5)

    def remote(src, dst, send, recv, peer):
        return pltpu.make_async_remote_copy(
            src_ref=src,
            dst_ref=dst,
            send_sem=send,
            recv_sem=recv,
            device_id=peer,
            device_id_type=pl.DeviceIdType.MESH,
        )

    def gather_copy(d):
        if d & 8:
            src, peer = d - 8, core
        elif d & 4:
            src, peer = d - 4, b_side
        elif d & 2:
            src, peer = d - 2, a_side
        else:
            src, peer = d - d % 2 if d > 16 else 0, z_side[1 if d % 2 else 2]
        return remote(rows.at[src], rows.at[d], ag_send.at[d], ag_recv.at[d], peer)

    def core_copy(j):
        src = part.at[j // 8 * 16 + 8 + j % 8]
        return remote(src, from_core.at[j], rs_send.at[j], rs_recv.at[j], core)

    def b_copy(j):
        src = part.at[j // 4 * 16 + 4 + j % 4]
        return remote(src, from_b.at[j], rs_send.at[16 + j], rs_recv.at[16 + j], b_side)

    def a_copy(j):
        src = part.at[j // 2 * 16 + 2 + j % 2]
        return remote(src, from_a.at[j], rs_send.at[24 + j], rs_recv.at[24 + j], a_side)

    def z_copy(k):
        src = part.at[k // 2 * 16 + k % 2]
        return remote(src, from_z.at[k], rs_send.at[28 + k], rs_recv.at[28 + k], z_side[2 - k % 2])

    width = wd.shape[1]
    tile = 256
    row_count = rows.shape[1]
    half = 16 * row_count

    def up_tile(first, n):
        span = pl.ds(first, 16)
        share = rows[span, :, width:].reshape(half, rows.shape[2] - width).astype(jnp.float32)
        lane = lax.broadcasted_iota(jnp.int32, share.shape, 1)
        share = jnp.sum(jnp.where(lane == e, share, 0.0), axis=1, keepdims=True)
        columns = pl.ds(n * tile, tile)
        x_rows = rows[span, :, :width].reshape(half, width)
        gate = jnp.dot(x_rows, wg[:, columns], preferred_element_type=jnp.float32)
        up = jnp.dot(x_rows, wu[:, columns], preferred_element_type=jnp.float32)
        act = gate / (1.0 + jnp.exp(-gate)) * up * share
        hidden[pl.ds(first * row_count, half), columns] = act.astype(jnp.bfloat16)

    def down(first):
        span = pl.ds(first, 8)

        def down_tile(n, _):
            columns = pl.ds(pl.multiple_of(n * 512, 512), 512)
            made = jnp.dot(
                hidden[pl.ds(first * row_count, half // 2)],
                wd[:, columns],
                preferred_element_type=jnp.float32,
            )
            part[span, :, columns] = made.astype(jnp.bfloat16).reshape(8, row_count, 512)
            return 0

        lax.fori_loop(0, width // 512, down_tile, 0)

    carried[...] = jnp.zeros_like(carried)

    def one_step(step, _):
        residual[...] = base[step]
        residual[:BLOCK] = residual[:BLOCK] + carried[...]
        held = residual[...]
        inverse = lax.rsqrt(jnp.mean(held * held, axis=1, keepdims=True) + 1e-06)
        rows[0, :, :width] = (held * inverse * gain[...]).astype(jnp.bfloat16)
        rows[0, :, width:] = tables[step]

        def forward(d):
            if d == 16:
                gather_copy(17).start()
            if d & 6 == 0:
                gather_copy(2 + d).start()
            if d & 4 == 0:
                gather_copy(4 + d).start()
            gather_copy(8 + d).start()

        def pass_on(*slots):
            for d in slots:
                gather_copy(d).wait_recv()
                forward(d)

        for d in (16, 1):
            gather_copy(d).start()
        forward(0)
        pass_on(2, 1, 4, 3, 5, 16, 6, 18, 7)

        @pl.when(step == 0)
        def _():
            for load in loads:
                load.wait()

        for d in range(8, 16):
            gather_copy(d).wait_recv()
        up_tile(0, 0)
        pass_on(17, 20)
        up_tile(0, 1)
        pass_on(19, 22, 21, 23)
        for d in range(24, SLOTS):
            gather_copy(d).wait_recv()
        up_tile(16, 0)
        up_tile(16, 1)
        for d in range(1, SLOTS):
            gather_copy(d).wait_send()

        def summed(z_half, r):
            j, mine = z_half * 8 + r, z_half * 16 + r
            core_copy(j).wait_recv()
            total = part[mine].astype(jnp.float32) + from_core[j].astype(jnp.float32)
            if r < 4:
                b_copy(z_half * 4 + r).wait_recv()
                total = total + from_b[z_half * 4 + r].astype(jnp.float32)
            if r < 2:
                a_copy(z_half * 2 + r).wait_recv()
                total = total + from_a[z_half * 2 + r].astype(jnp.float32)
            if (z_half, r) == (1, 0):
                z_copy(3).wait_recv()
                total = total + from_z[3].astype(jnp.float32)
            return total

        def hand_on(z_half, *places):
            for r in places:
                part[z_half * 16 + r] = summed(z_half, r).astype(jnp.bfloat16)
                if r >= 4:
                    b_copy(z_half * 4 + r - 4).start()
                elif r >= 2:
                    a_copy(z_half * 2 + r - 2).start()
                else:
                    z_copy(z_half * 2 + r).start()

        order = (7, 5, 6, 4, 3, 1, 2, 0)
        down(24)
        for r in order:
            core_copy(8 + r).start()
        down(16)
        hand_on(1, 7, 5, 6, 4)
        down(8)
        for r in order:
            core_copy(r).start()
        hand_on(1, 3)
        down(0)
        hand_on(0, 7, 5)
        hand_on(1, 2, 1)
        hand_on(0, 6, 4)
        hand_on(1, 0)
        hand_on(0, 3, 2, 1)
        total = summed(0, 0)
        for k in (1, 2):
            z_copy(k).wait_recv()
            total = total + from_z[k].astype(jnp.float32)
        result = (residual[...] + total).astype(jnp.bfloat16)
        out[step] = result
        carried[...] = result.astype(jnp.float32)[:BLOCK]
        for j in range(16):
            core_copy(j).wait_send()
        for j in range(8):
            b_copy(j).wait_send()
        for j in range(4):
            a_copy(j).wait_send()
        for k in (1, 2, 3):
            z_copy(k).wait_send()
        return 0

    lax.fori_loop(0, 2, one_step, 0)


def on_device_close(
    cache_keys, cache_values, lengths, drift_rows, block_in, drift_in, queries, new_keys,
    new_values, norm_gain, expert_ids, gate_weights, w_gate, w_up, w_down,
):
    base = attend_both(
        cache_keys[0],
        cache_values[0],
        lengths[0],
        drift_rows[:, 0],
        queries[:, 0],
        new_keys[:, 0],
        new_values[:, 0],
        block_in[0],
        drift_in[:, 0],
    )
    row_count, width = queries.shape[2], queries.shape[3]
    member = expert_ids[:, 0, :, :, None] == jnp.arange(128)
    tables = jnp.sum(jnp.where(member, gate_weights[:, 0, :, :, None], 0), axis=2)
    tables = tables.astype(jnp.bfloat16)
    vmem = pl.BlockSpec(memory_space=pltpu.VMEM)
    hbm = pl.BlockSpec(memory_space=pl.ANY)
    block = (row_count, width)
    bf16 = jnp.bfloat16
    out = pl.pallas_call(
        expert_kernel,
        out_shape=jax.ShapeDtypeStruct((2, row_count, width), bf16),
        in_specs=[vmem, vmem, vmem, hbm, hbm, hbm],
        out_specs=vmem,
        scratch_shapes=[
            pltpu.VMEM((SLOTS, row_count, width + 128), bf16),
            pltpu.VMEM((SLOTS, *block), bf16),
            pltpu.VMEM((SLOTS * row_count, w_down.shape[1]), bf16),
            pltpu.VMEM((16, *block), bf16),
            pltpu.VMEM((8, *block), bf16),
            pltpu.VMEM((4, *block), bf16),
            pltpu.VMEM((4, *block), bf16),
            pltpu.VMEM(block, jnp.float32),
            pltpu.VMEM((BLOCK, width), jnp.float32),
            pltpu.VMEM(w_gate.shape[1:], bf16),
            pltpu.VMEM(w_up.shape[1:], bf16),
            pltpu.VMEM(w_down.shape[1:], bf16),
            pltpu.SemaphoreType.DMA((3,)),
            pltpu.SemaphoreType.DMA((SLOTS,)),
            pltpu.SemaphoreType.DMA((SLOTS,)),
            pltpu.SemaphoreType.DMA((SLOTS,)),
            pltpu.SemaphoreType.DMA((SLOTS,)),
        ],
        compiler_params=pltpu.CompilerParams(
            collective_id=0, has_side_effects=True, vmem_limit_bytes=60 * 2**20
        ),
        name="experts",
    )(base, tables, norm_gain[None], w_gate[0], w_up[0], w_down[0])
    return out[:, None]


def solution(mesh):
    close = mesh.shape["rep"] == 2 and mesh.shape["exp"] == 16
    placed = (
        P(("rep", "exp"), None, None),
        P(("rep", "exp"), None, None),
        P(("rep", "exp")),
        P(None, ("rep", "exp"), None),
        P(("rep", "exp"), None, None),
        P(None, ("rep", "exp"), None, None),
        P(None, ("rep", "exp"), None, None),
        P(None, ("rep", "exp"), None, None),
        P(None, ("rep", "exp"), None, None),
        P(),
        P(None, ("rep", "exp"), None, None),
        P(None, ("rep", "exp"), None, None),
        P("exp", None, "rep"),
        P("exp", None, "rep"),
        P("exp", "rep", None),
    )
    return jax.shard_map(
        on_device_close if close else on_device,
        mesh=mesh,
        in_specs=placed,
        out_specs=P(None, ("rep", "exp"), None, None),
        check_vma=False,
    )
```

```python
import jax
import jax.numpy as jnp
from jax import lax
from jax.experimental import pallas as pl
from jax.experimental.pallas import tpu as pltpu
from jax.sharding import PartitionSpec as P

H = 32
KVH = 4
HD = 128
TOP = 8
BLOCK = 8


def attend(query_rows, key_rows, value_rows, block_keys, block_values, length):
    row_count = query_rows.shape[0]
    group_size = H // KVH
    query_head_rows = query_rows.reshape(row_count, KVH, group_size, HD)
    cache_k = key_rows.reshape(-1, KVH, HD)
    cached_value_rows = value_rows.reshape(-1, KVH, HD)
    prompt_key_rows = block_keys.reshape(-1, KVH, HD)
    prompt_value_rows = block_values.reshape(-1, KVH, HD)
    logit_scale_factor = HD ** (-0.5)
    cache_scores = (
        jnp.einsum("rkgd,ckd->kgrc", query_head_rows, cache_k, preferred_element_type=jnp.float32)
        * logit_scale_factor
    )
    prompt_score_rows = (
        jnp.einsum(
            "afhu,nfu->fhan", query_head_rows, prompt_key_rows, preferred_element_type=jnp.float32
        )
        * logit_scale_factor
    )
    cache_mask = jnp.arange(cache_k.shape[0]) < length
    own_mask = (jnp.arange(row_count) < BLOCK)[:, None]
    cache_scores = jnp.where(cache_mask, cache_scores, -1e30)
    prompt_score_rows = jnp.where(own_mask, prompt_score_rows, -1e30)
    peak = jnp.maximum(jnp.max(cache_scores, axis=-1), jnp.max(prompt_score_rows, axis=-1))
    cache_exp = jnp.exp(cache_scores - peak[..., None])
    own_exp = jnp.exp(prompt_score_rows - peak[..., None])
    denom = jnp.sum(cache_exp, axis=-1) + jnp.sum(own_exp, axis=-1)
    cached_weight_share = (cache_exp / denom[..., None]).astype(jnp.bfloat16)
    prompt_weight_share = (own_exp / denom[..., None]).astype(jnp.bfloat16)
    blended_output = jnp.einsum(
        "qimt,tqj->mqij", cached_weight_share, cached_value_rows, preferred_element_type=jnp.float32
    )
    blended_output = blended_output + jnp.einsum(
        "iywf,fie->wiye", prompt_weight_share, prompt_value_rows, preferred_element_type=jnp.float32
    )
    return blended_output.reshape(row_count, H * HD)


def route_table(routed, gate_share, experts, capacity):
    member = routed[:, :, None] == jnp.arange(experts)[None, None, :]
    weight = jnp.sum(jnp.where(member, gate_share[:, :, None].astype(jnp.float32), 0.0), axis=1)
    chosen = jnp.any(member, axis=1).astype(jnp.int32)
    slot_rank = jnp.cumsum(chosen, axis=0) - chosen
    taken = (slot_rank[:, :, None] == jnp.arange(capacity)[None, None, :]) & (
        chosen[:, :, None] == 1
    )
    return jnp.where(taken, weight[:, :, None], 0.0).astype(jnp.bfloat16)


def expert_terms(routed_rows, gate_part, up_part, down_part):
    flat_rows = routed_rows.reshape(-1, routed_rows.shape[-1])
    gate_act = jnp.dot(flat_rows, gate_part, preferred_element_type=jnp.float32)
    up_act = jnp.dot(flat_rows, up_part, preferred_element_type=jnp.float32)
    hidden = (jax.nn.silu(gate_act) * up_act).astype(jnp.bfloat16)
    produced = jnp.dot(hidden, down_part, preferred_element_type=jnp.float32).astype(jnp.bfloat16)
    return produced.reshape(routed_rows.shape)


def on_device(
    cache_keys,
    cache_values,
    lengths,
    drift_rows,
    block_in,
    drift_in,
    queries,
    new_keys,
    new_values,
    norm_gain,
    expert_ids,
    gate_weights,
    w_gate,
    w_up,
    w_down,
):
    rep_count = lax.axis_size("rep")
    experts = lax.axis_size("exp") * w_gate.shape[0]
    row_count = queries.shape[2]
    capacity = min(row_count, (3 * row_count * TOP + 2 * experts - 1) // (2 * experts))
    key_rows = cache_keys[0]
    value_rows = cache_values[0]
    carried = block_in[0]
    results = []
    for denoise in range(2):
        key_rows = key_rows.at[drift_rows[denoise, 0]].set(new_keys[denoise, 0, BLOCK:])
        value_rows = value_rows.at[drift_rows[denoise, 0]].set(new_values[denoise, 0, BLOCK:])
        attended = attend(
            queries[denoise, 0],
            key_rows,
            value_rows,
            new_keys[denoise, 0, :BLOCK],
            new_values[denoise, 0, :BLOCK],
            lengths[0],
        )
        inputs = jnp.concatenate([carried, drift_in[denoise, 0]], axis=0).astype(jnp.float32)
        residual = inputs + attended
        inverse = lax.rsqrt(jnp.mean(residual * residual, axis=-1, keepdims=True) + 1e-06)
        normed = (residual * inverse * norm_gain).astype(jnp.bfloat16)
        slot_table = route_table(
            expert_ids[denoise, 0], gate_weights[denoise, 0], experts, capacity
        )
        flat_table = slot_table.reshape(row_count, experts * capacity)
        all_rows, all_tables = (
            lax.all_gather(normed, "rep", axis=0, tiled=True),
            lax.all_gather(flat_table, "rep", axis=0, tiled=True),
        )
        all_rows = all_rows.reshape(rep_count, row_count, -1)
        all_tables = all_tables.reshape(rep_count, row_count, experts, capacity)
        chosen_slots = (all_tables != 0).astype(jnp.bfloat16)
        dispatched = jnp.einsum(
            "orec,ord->eocd", chosen_slots, all_rows, preferred_element_type=jnp.float32
        ).astype(jnp.bfloat16)
        produced = expert_terms(
            lax.all_to_all(dispatched, "exp", split_axis=0, concat_axis=0, tiled=True),
            w_gate[0],
            w_up[0],
            w_down[0],
        )
        expert_out = lax.all_to_all(produced, "exp", split_axis=0, concat_axis=0, tiled=True)
        combined = jnp.einsum(
            "orec,eocd->ord", all_tables, expert_out, preferred_element_type=jnp.float32
        )
        moe = lax.psum_scatter(
            combined.reshape(rep_count * row_count, -1).astype(jnp.bfloat16),
            "rep",
            scatter_dimension=0,
            tiled=True,
        ).astype(jnp.float32)
        result = (residual + moe).astype(jnp.bfloat16)
        results.append(result)
        carried = result[:BLOCK]
    return jnp.stack(results)[:, None]


GROUP = H // KVH


def attention_kernel(
    q_ref, k_ref, v_ref, nk_ref, nv_ref, mask_ref, xmask_ref, first_ref, drift_ref, out_ref
):
    scale = HD ** (-0.5)
    keys, values = k_ref[...], v_ref[...]
    row_count = q_ref.shape[1]
    for step in range(2):
        q = jnp.concatenate(
            [q_ref[step, :, g * HD : (g + 1) * HD] for g in range(GROUP)], axis=0
        )
        nt = (((1,), (1,)), ((), ()))
        scores = lax.dot_general(q, keys, nt, preferred_element_type=jnp.float32)
        scores = scores * scale + mask_ref[step]
        extra_keys = jnp.concatenate([nk_ref[step], nk_ref[0]], axis=0)
        extra_values = jnp.concatenate([nv_ref[step], nv_ref[0]], axis=0)
        extra = lax.dot_general(q, extra_keys, nt, preferred_element_type=jnp.float32)
        extra = extra * scale + xmask_ref[step]
        peak = jnp.maximum(
            jnp.max(scores, axis=1, keepdims=True), jnp.max(extra, axis=1, keepdims=True)
        )
        scores = jnp.exp(scores - peak)
        extra = jnp.exp(extra - peak)
        denom = jnp.sum(scores, axis=1, keepdims=True) + jnp.sum(extra, axis=1, keepdims=True)
        mixed = jnp.dot(scores.astype(jnp.bfloat16), values, preferred_element_type=jnp.float32)
        mixed += jnp.dot(
            extra.astype(jnp.bfloat16), extra_values, preferred_element_type=jnp.float32
        )
        mixed = mixed / denom
        for g in range(GROUP):
            columns = slice(g * HD, (g + 1) * HD)
            block = mixed[g * row_count : g * row_count + BLOCK]
            if step == 0:
                block = block + first_ref[:, columns].astype(jnp.float32)
            drifted = mixed[g * row_count + BLOCK : (g + 1) * row_count]
            out_ref[step, :BLOCK, columns] = block
            out_ref[step, BLOCK:, columns] = drifted + drift_ref[step, :, columns].astype(jnp.float32)


def attend_both(keys, values, length, drift, queries, new_keys, new_values, first, drift_in):
    row_count, slots = queries.shape[1], keys.shape[0]
    places = jnp.arange(slots)
    hit = jnp.any(places[None, None, :] == drift[:, :, None], axis=1)
    valid = places < length
    open_ = jnp.stack([valid & ~hit[0], valid & ~hit[0] & ~hit[1]])
    mask = jnp.where(open_, 0.0, -1e30).astype(jnp.float32)[:, None, :]
    kept = ~jnp.any(drift[0][:, None] == drift[1][None, :], axis=1)
    own = (jnp.arange(row_count) < BLOCK)[None, :, None]
    own = jnp.broadcast_to(own, (2, row_count, BLOCK))
    fresh = jnp.ones((2, row_count, row_count - BLOCK), bool)
    older = jnp.stack([jnp.zeros_like(kept), kept])[:, None, :]
    older = jnp.broadcast_to(older, (2, row_count, kept.shape[0]))
    none = jnp.zeros((2, row_count, BLOCK), bool)
    xmask = jnp.where(jnp.concatenate([own, fresh, none, older], axis=2), 0.0, -1e30)
    xmask = jnp.tile(xmask.astype(jnp.float32), (1, GROUP, 1))

    wide = GROUP * HD
    return pl.pallas_call(
        attention_kernel,
        grid=(KVH,),
        in_specs=[
            pl.BlockSpec((2, row_count, wide), lambda j: (0, 0, j)),
            pl.BlockSpec((slots, HD), lambda j: (0, j)),
            pl.BlockSpec((slots, HD), lambda j: (0, j)),
            pl.BlockSpec((2, row_count, HD), lambda j: (0, 0, j)),
            pl.BlockSpec((2, row_count, HD), lambda j: (0, 0, j)),
            pl.BlockSpec((2, 1, slots), lambda j: (0, 0, 0)),
            pl.BlockSpec((2, GROUP * row_count, 2 * row_count), lambda j: (0, 0, 0)),
            pl.BlockSpec((BLOCK, wide), lambda j: (0, j)),
            pl.BlockSpec((2, row_count - BLOCK, wide), lambda j: (0, 0, j)),
        ],
        out_specs=pl.BlockSpec((2, row_count, wide), lambda j: (0, 0, j)),
        out_shape=jax.ShapeDtypeStruct((2, row_count, H * HD), jnp.float32),
        compiler_params=pltpu.CompilerParams(vmem_limit_bytes=60 * 2**20),
        name="attention",
    )(queries, keys, values, new_keys, new_values, mask, xmask, first, drift_in)


SLOTS = 32


def expert_kernel(
    base, tables, gain, wg_in, wu_in, wd_in, out,
    rows, part, hidden, from_core, from_b, from_a, from_z, residual, carried, wg, wu, wd,
    w_sem, ag_send, ag_recv, rs_send, rs_recv,
):
    y, e = lax.axis_index("rep"), lax.axis_index("exp")
    c, x, z = lax.rem(e, 2), lax.rem(lax.div(e, 2), 2), lax.div(e, 4)
    z_low, z_high = lax.rem(z, 2), lax.div(z, 2)

    def device(y_, z_, x_, c_):
        return (y_, (z_ * 2 + x_) * 2 + c_)

    core = device(y, z, x, 1 - c)
    a_side = device(y + c * (1 - 2 * y), z, x + (1 - c) * (1 - 2 * x), c)
    b_side = device(y + (1 - c) * (1 - 2 * y), z, x + c * (1 - 2 * x), c)
    z_side = [None] + [
        device(
            y,
            ((1 - z_high) if k & 2 else z_high) * 2 + ((1 - z_low) if k & 1 else z_low),
            x,
            c,
        )
        for k in (1, 2)
    ]

    loads = [
        pltpu.make_async_copy(src, dst, w_sem.at[i])
        for i, (src, dst) in enumerate(((wg_in, wg), (wu_in, wu), (wd_in, wd)))
    ]
    for load in loads:
        load.start()

    barrier = pltpu.get_barrier_semaphore()
    for peer in (core, a_side, b_side, *z_side[1:]):
        pl.semaphore_signal(barrier, inc=1, device_id=peer, device_id_type=pl.DeviceIdType.MESH)
    pl.semaphore_wait(barrier, 5)

    def remote(src, dst, send, recv, peer):
        return pltpu.make_async_remote_copy(
            src_ref=src,
            dst_ref=dst,
            send_sem=send,
            recv_sem=recv,
            device_id=peer,
            device_id_type=pl.DeviceIdType.MESH,
        )

    def gather_copy(d):
        if d & 8:
            src, peer = d - 8, core
        elif d & 4:
            src, peer = d - 4, b_side
        elif d & 2:
            src, peer = d - 2, a_side
        else:
            src, peer = d - d % 2 if d > 16 else 0, z_side[1 if d % 2 else 2]
        return remote(rows.at[src], rows.at[d], ag_send.at[d], ag_recv.at[d], peer)

    def core_copy(j):
        src = part.at[j // 8 * 16 + 8 + j % 8]
        return remote(src, from_core.at[j], rs_send.at[j], rs_recv.at[j], core)

    def b_copy(j):
        src = part.at[j // 4 * 16 + 4 + j % 4]
        return remote(src, from_b.at[j], rs_send.at[16 + j], rs_recv.at[16 + j], b_side)

    def a_copy(j):
        src = part.at[j // 2 * 16 + 2 + j % 2]
        return remote(src, from_a.at[j], rs_send.at[24 + j], rs_recv.at[24 + j], a_side)

    def z_copy(k):
        src = part.at[k // 2 * 16 + k % 2]
        return remote(src, from_z.at[k], rs_send.at[28 + k], rs_recv.at[28 + k], z_side[2 - k % 2])

    width = wd.shape[1]
    tile = 256
    row_count = rows.shape[1]
    half = 16 * row_count

    def up_tile(first, n):
        span = pl.ds(first, 16)
        share = rows[span, :, width:].reshape(half, rows.shape[2] - width).astype(jnp.float32)
        lane = lax.broadcasted_iota(jnp.int32, share.shape, 1)
        share = jnp.sum(jnp.where(lane == e, share, 0.0), axis=1, keepdims=True)
        columns = pl.ds(n * tile, tile)
        x_rows = rows[span, :, :width].reshape(half, width)
        gate = jnp.dot(x_rows, wg[:, columns], preferred_element_type=jnp.float32)
        up = jnp.dot(x_rows, wu[:, columns], preferred_element_type=jnp.float32)
        act = gate / (1.0 + jnp.exp(-gate)) * up * share
        hidden[pl.ds(first * row_count, half), columns] = act.astype(jnp.bfloat16)

    def down(first):
        span = pl.ds(first, 8)

        def down_tile(n, _):
            columns = pl.ds(pl.multiple_of(n * 512, 512), 512)
            made = jnp.dot(
                hidden[pl.ds(first * row_count, half // 2)],
                wd[:, columns],
                preferred_element_type=jnp.float32,
            )
            part[span, :, columns] = made.astype(jnp.bfloat16).reshape(8, row_count, 512)
            return 0

        lax.fori_loop(0, width // 512, down_tile, 0)

    carried[...] = jnp.zeros_like(carried)

    def one_step(step, _):
        residual[...] = base[step]
        residual[:BLOCK] = residual[:BLOCK] + carried[...]
        held = residual[...]
        inverse = lax.rsqrt(jnp.mean(held * held, axis=1, keepdims=True) + 1e-06)
        rows[0, :, :width] = (held * inverse * gain[...]).astype(jnp.bfloat16)
        rows[0, :, width:] = tables[step]

        def forward(d):
            if d == 16:
                gather_copy(17).start()
            if d & 6 == 0:
                gather_copy(2 + d).start()
            if d & 4 == 0:
                gather_copy(4 + d).start()
            gather_copy(8 + d).start()

        def pass_on(*slots):
            for d in slots:
                gather_copy(d).wait_recv()
                forward(d)

        for d in (16, 1):
            gather_copy(d).start()
        forward(0)
        pass_on(2, 1, 16, 3, 18, 17, 4, 5, 19, 6, 7)

        @pl.when(step == 0)
        def _():
            for load in loads:
                load.wait()

        for d in range(8, 16):
            gather_copy(d).wait_recv()
        up_tile(0, 0)
        pass_on(20, 22)
        up_tile(0, 1)
        pass_on(21, 23)
        down(8)
        down(0)
        for d in range(24, SLOTS):
            gather_copy(d).wait_recv()
        up_tile(16, 0)
        up_tile(16, 1)
        for d in range(1, SLOTS):
            gather_copy(d).wait_send()

        def summed(z_half, r):
            j, mine = z_half * 8 + r, z_half * 16 + r
            core_copy(j).wait_recv()
            total = part[mine].astype(jnp.float32) + from_core[j].astype(jnp.float32)
            if r < 4:
                b_copy(z_half * 4 + r).wait_recv()
                total = total + from_b[z_half * 4 + r].astype(jnp.float32)
            if r < 2:
                a_copy(z_half * 2 + r).wait_recv()
                total = total + from_a[z_half * 2 + r].astype(jnp.float32)
            if (z_half, r) == (1, 0):
                z_copy(3).wait_recv()
                total = total + from_z[3].astype(jnp.float32)
            return total

        def hand_on(z_half, *places):
            for r in places:
                part[z_half * 16 + r] = summed(z_half, r).astype(jnp.bfloat16)
                if r >= 4:
                    b_copy(z_half * 4 + r - 4).start()
                elif r >= 2:
                    a_copy(z_half * 2 + r - 2).start()
                else:
                    z_copy(z_half * 2 + r).start()

        order = (7, 5, 6, 4, 3, 1, 2, 0)
        down(24)
        for r in order:
            core_copy(8 + r).start()
        down(16)
        hand_on(1, 7, 5, 6, 4)
        for r in order:
            core_copy(r).start()
        hand_on(0, 7, 5)
        hand_on(1, 3)
        hand_on(1, 2, 1)
        hand_on(0, 6, 4)
        hand_on(1, 0)
        hand_on(0, 3, 2, 1)
        total = summed(0, 0)
        for k in (1, 2):
            z_copy(k).wait_recv()
            total = total + from_z[k].astype(jnp.float32)
        result = (residual[...] + total).astype(jnp.bfloat16)
        out[step] = result
        carried[...] = result.astype(jnp.float32)[:BLOCK]
        for j in range(16):
            core_copy(j).wait_send()
        for j in range(8):
            b_copy(j).wait_send()
        for j in range(4):
            a_copy(j).wait_send()
        for k in (1, 2, 3):
            z_copy(k).wait_send()
        return 0

    lax.fori_loop(0, 2, one_step, 0)


def on_device_close(
    cache_keys, cache_values, lengths, drift_rows, block_in, drift_in, queries, new_keys,
    new_values, norm_gain, expert_ids, gate_weights, w_gate, w_up, w_down,
):
    base = attend_both(
        cache_keys[0],
        cache_values[0],
        lengths[0],
        drift_rows[:, 0],
        queries[:, 0],
        new_keys[:, 0],
        new_values[:, 0],
        block_in[0],
        drift_in[:, 0],
    )
    row_count, width = queries.shape[2], queries.shape[3]
    member = expert_ids[:, 0, :, :, None] == jnp.arange(128)
    tables = jnp.sum(jnp.where(member, gate_weights[:, 0, :, :, None], 0), axis=2)
    tables = tables.astype(jnp.bfloat16)
    vmem = pl.BlockSpec(memory_space=pltpu.VMEM)
    hbm = pl.BlockSpec(memory_space=pl.ANY)
    block = (row_count, width)
    bf16 = jnp.bfloat16
    out = pl.pallas_call(
        expert_kernel,
        out_shape=jax.ShapeDtypeStruct((2, row_count, width), bf16),
        in_specs=[vmem, vmem, vmem, hbm, hbm, hbm],
        out_specs=vmem,
        scratch_shapes=[
            pltpu.VMEM((SLOTS, row_count, width + 128), bf16),
            pltpu.VMEM((SLOTS, *block), bf16),
            pltpu.VMEM((SLOTS * row_count, w_down.shape[1]), bf16),
            pltpu.VMEM((16, *block), bf16),
            pltpu.VMEM((8, *block), bf16),
            pltpu.VMEM((4, *block), bf16),
            pltpu.VMEM((4, *block), bf16),
            pltpu.VMEM(block, jnp.float32),
            pltpu.VMEM((BLOCK, width), jnp.float32),
            pltpu.VMEM(w_gate.shape[1:], bf16),
            pltpu.VMEM(w_up.shape[1:], bf16),
            pltpu.VMEM(w_down.shape[1:], bf16),
            pltpu.SemaphoreType.DMA((3,)),
            pltpu.SemaphoreType.DMA((SLOTS,)),
            pltpu.SemaphoreType.DMA((SLOTS,)),
            pltpu.SemaphoreType.DMA((SLOTS,)),
            pltpu.SemaphoreType.DMA((SLOTS,)),
        ],
        compiler_params=pltpu.CompilerParams(
            collective_id=0, has_side_effects=True, vmem_limit_bytes=60 * 2**20
        ),
        name="experts",
    )(base, tables, norm_gain[None], w_gate[0], w_up[0], w_down[0])
    return out[:, None]


def solution(mesh):
    close = mesh.shape["rep"] == 2 and mesh.shape["exp"] == 16
    placed = (
        P(("rep", "exp"), None, None),
        P(("rep", "exp"), None, None),
        P(("rep", "exp")),
        P(None, ("rep", "exp"), None),
        P(("rep", "exp"), None, None),
        P(None, ("rep", "exp"), None, None),
        P(None, ("rep", "exp"), None, None),
        P(None, ("rep", "exp"), None, None),
        P(None, ("rep", "exp"), None, None),
        P(),
        P(None, ("rep", "exp"), None, None),
        P(None, ("rep", "exp"), None, None),
        P("exp", None, "rep"),
        P("exp", None, "rep"),
        P("exp", "rep", None),
    )
    return jax.shard_map(
        on_device_close if close else on_device,
        mesh=mesh,
        in_specs=placed,
        out_specs=P(None, ("rep", "exp"), None, None),
        check_vma=False,
    )
```
